128 devices in a mesh: node: 8 (over z, y_lo), local: 16 (over x, y_hi, core).
Axes of the slice: x: 4, y: 4 (y_hi: 2, y_lo: 2; y = y_hi * 2 + y_lo), z: 4, core: 2. Of those that a mesh axis runs over, the one named last changes fastest.
Arguments:
- tokens: bfloat16 [16384, 2048], P(('node', 'local')), may hold values from -24 to 24
- expert_ids: int32 [16384, 2], P(('node', 'local')), may hold values from 0 to 127, as said below
- gate_code: int32 [16384], P(('node', 'local')), may hold values from 1 to 7
- grad_out: bfloat16 [16384, 2048], P(('node', 'local')), may hold values from -3 to 3
- up_weight: bfloat16 [128, 2048, 1024], P(('node', 'local')), may hold values from -0.125 to 0.125
- down_weight: bfloat16 [128, 1024, 2048], P(('node', 'local')), may hold values from -0.1875 to 0.1875
- shared_up: bfloat16 [2048, 1024], P('local'), may hold values from -0.125 to 0.125
- shared_down: bfloat16 [1024, 2048], P('local'), may hold values from -0.1875 to 0.1875
Outputs:
- layer_out: bfloat16 [16384, 2048], P(('node', 'local'))
- grad_tokens: bfloat16 [16384, 2048], P(('node', 'local'))
- grad_up: bfloat16 [128, 2048, 1024], P(('node', 'local'))
- grad_down: bfloat16 [128, 1024, 2048], P(('node', 'local'))
- grad_shared_up: float32 [2048, 1024], P('local')
- grad_shared_down: float32 [1024, 2048], P('local')
The draws below stay inside these ranges and needn't reach their ends.
Inputs may be any that keep to these rules, and one draw needn't show every extreme that they name: `expert_ids`: each token names two different experts. In each block of 128 consecutive tokens no expert is named by more than 4 tokens, and one expert, the same in every block, is named by exactly 4 tokens of every block.
All inputs are finite; a program needn't handle non-finite values.
Results may differ from the reference program's by a relative error of at most 0.0058.
Values may be sent and summed in bfloat16 or wider, within the bound.
No kernel may reach another device: no remote copies, remote signals or barrier semaphores. Data moves between devices by JAX's collectives and lax.ppermute only.
A program may use at most 128 MiB of HBM per device.

```python
import jax
import jax.numpy as jnp
from jax import lax

D = 2048
H = 1024
HS = 1024
TOK_DEV = 128
EXPERTS = 128
CAP = 4
TOKENS = 16384
N_NODE = 8
N_LOCAL = 16


def block_routes(block_key, busiest):
    subkeys = jax.random.split(block_key, 5)
    others = (busiest + 1 + jax.random.permutation(subkeys[0], EXPERTS - 1)) % EXPERTS
    first_count = (EXPERTS - 1) // 2
    second_count = EXPERTS - 1 - first_count
    ranking = jax.random.permutation(subkeys[1], TOK_DEV)
    pick_first = jax.random.permutation(subkeys[2], first_count * CAP)[:TOK_DEV] // CAP
    pick_second = jax.random.permutation(subkeys[3], second_count * CAP)[:TOK_DEV] // CAP
    column_one = jnp.where(ranking < CAP, busiest, others[pick_first])
    column_two = others[first_count + pick_second]
    flipped = jax.random.randint(subkeys[4], (TOK_DEV,), 0, 2)
    leading = jnp.where(flipped == 1, column_two, column_one)
    trailing = jnp.where(flipped == 1, column_one, column_two)
    return jnp.stack([leading, trailing], axis=1)


def draw_expert_ids(key, part):
    key = jax.random.fold_in(key, 7)
    busy_key, rest_key = jax.random.split(key)
    busiest = jax.random.randint(busy_key, (), 0, EXPERTS)
    block_keys = jax.random.split(rest_key, TOKENS // TOK_DEV)
    routes = jax.vmap(block_routes, in_axes=(0, None))(block_keys, busiest)
    return routes.reshape(TOKENS, 2).astype(jnp.int32)


def with_ends(drawn, stream_key, least, high):
    spot = [jax.random.randint(jax.random.fold_in(stream_key, axis), (), 0, length) for axis, length in enumerate(drawn.shape)]
    longest = drawn.shape.index(max(drawn.shape))
    next_to = spot[:longest] + [(spot[longest] + 1) % drawn.shape[longest]] + spot[longest + 1:]
    return drawn.at[tuple(spot)].set(least).at[tuple(next_to)].set(high)


def with_spikes(entries, rng, source, target, shards_of, factor):
    owner, partner = [(jnp.arange(entries.shape[dim]) // (entries.shape[dim] // shards_of)).reshape([-1 if axis == dim else 1 for axis in range(entries.ndim)]) for dim in (source, target)]
    chosen = jax.random.permutation(rng, shards_of)[partner]
    strong = (owner == chosen) | (owner == (partner + shards_of // 2) % shards_of)
    return jnp.where(strong, factor * entries, entries)


def steps_of(key, dims, shards, smallest, largest):
    level = 1.0
    for axis_at, parts in shards:
        draws = jax.random.uniform(jax.random.fold_in(jax.random.fold_in(key, 6), axis_at), (parts,), jnp.float32, smallest / len(shards), largest / len(shards))
        level = level * jnp.repeat(jnp.exp(draws), dims[axis_at] // parts).reshape((-1,) + (1,) * (len(dims) - 1 - axis_at))
    return level


def gaussian(rng, shape, scale, limit, cuts=(), kind=jnp.bfloat16):
    level = steps_of(rng, shape, cuts, -0.22, 0.18) if cuts else 1.0
    values = jax.random.normal(rng, shape, jnp.float32) * scale * level
    return jnp.minimum(jnp.maximum(values, -limit), limit).astype(kind)


def bell_draw_with(key, dims, scale, limit, cuts, heavy, kind=jnp.bfloat16):
    values = scale * jax.random.normal(key, dims, jnp.float32)
    if cuts:
        values = values * steps_of(key, dims, cuts, -0.22, 0.18)
    return jnp.clip(with_spikes(values, jax.random.fold_in(key, 3), *heavy), -limit, limit).astype(kind)


def setup_inputs(seed: int = 0) -> dict:
    key_of = jax.random.split(jax.random.key(seed), 9)
    return {
        "tokens": bell_draw_with(key_of[0], (TOKENS, D), 1.0, 24.0, ((0, 128),), (0, 1, 128, 5.5)),
        "expert_ids": draw_expert_ids(jax.random.fold_in(key_of[8], 71), 0),
        "gate_code": with_ends(jax.random.randint(key_of[2], (TOKENS,), 1, 8), jax.random.fold_in(key_of[2], 1), 1, 7).astype(jnp.int32),
        "grad_out": gaussian(key_of[3], (TOKENS, D), 0.5, 3.0, ((0, 128),)),
        "up_weight": gaussian(key_of[4], (EXPERTS, D, H), D ** -0.5, 0.125, ((0, 128),)),
        "down_weight": gaussian(key_of[5], (EXPERTS, H, D), H ** -0.5, 0.1875, ((0, 128),)),
        "shared_up": gaussian(key_of[6], (D, HS), D ** -0.5, 0.125, ((0, 16),)),
        "shared_down": gaussian(key_of[7], (HS, D), HS ** -0.5, 0.1875, ((0, 16),)),
    }


half_root = 0.7071067811865476
inv_root_tau = 0.3989422804014327


def gelu_value(values):
    return 0.5 * values * (1.0 + lax.erf(values * half_root))


def gelu_slope(values):
    return 0.5 * (1.0 + lax.erf(values * half_root)) + values * inv_root_tau * jnp.exp(-0.5 * values * values)


def reference(tokens, expert_ids, gate_code, grad_out, up_weight, down_weight, shared_up, shared_down):
    devices = N_NODE * N_LOCAL
    per_expert = devices * CAP
    first_gate = gate_code.astype(jnp.float32) / 8.0
    gate_pairs = jnp.stack([first_gate, 1.0 - first_gate], axis=1)
    blocked_ids = expert_ids.reshape(devices, 2 * TOK_DEV)
    onehot = (blocked_ids[:, :, None] == jnp.arange(EXPERTS, dtype=jnp.int32)[None, None, :]).astype(jnp.int32)
    before = jnp.cumsum(onehot, axis=1) - onehot
    position = jnp.sum(before * onehot, axis=2)
    source = jnp.arange(devices, dtype=jnp.int32)[:, None]
    slot_row = (source * CAP + position).reshape(-1).astype(jnp.int32)
    expert = expert_ids.reshape(-1).astype(jnp.int32)
    token_ids = jnp.repeat(jnp.arange(TOKENS, dtype=jnp.int32), 2)
    token_table = jnp.zeros((EXPERTS, per_expert), jnp.int32).at[expert, slot_row].set(token_ids)
    filled = jnp.zeros((EXPERTS, per_expert), jnp.float32).at[expert, slot_row].set(1.0)
    gate_table = jnp.zeros((EXPERTS, per_expert), jnp.float32).at[expert, slot_row].set(gate_pairs.reshape(-1))

    def one_expert(packed):
        upward, downward, picks, filled_rows, gating = packed
        picked = jnp.where(filled_rows[:, None] > 0, tokens[picks], jnp.zeros((), tokens.dtype))
        preact = jnp.dot(picked, upward, preferred_element_type=jnp.float32)
        hidden = gelu_value(preact).astype(jnp.bfloat16)
        result = jnp.dot(hidden, downward, preferred_element_type=jnp.float32).astype(jnp.bfloat16)
        upstream = (gating[:, None] * grad_out[picks].astype(jnp.float32)).astype(jnp.bfloat16)
        hidden_grad = jnp.dot(upstream, downward.T, preferred_element_type=jnp.float32)
        slopes = (hidden_grad * gelu_slope(preact)).astype(jnp.bfloat16)
        grad_lower = jnp.dot(hidden.T, upstream, preferred_element_type=jnp.float32).astype(jnp.bfloat16)
        grad_upper = jnp.dot(picked.T, slopes, preferred_element_type=jnp.float32).astype(jnp.bfloat16)
        inward = jnp.dot(slopes, upward.T, preferred_element_type=jnp.float32).astype(jnp.bfloat16)
        return result, inward, grad_upper, grad_lower

    results, inwards, grad_up, grad_down = lax.map(one_expert, (up_weight, down_weight, token_table, filled, gate_table))
    routed = results[expert, slot_row].astype(jnp.float32).reshape(TOKENS, 2, D)
    routed_out = jnp.sum(gate_pairs[:, :, None] * routed, axis=1)
    routed_grad = jnp.sum(inwards[expert, slot_row].astype(jnp.float32).reshape(TOKENS, 2, D), axis=1)
    shared_pre = jnp.dot(tokens, shared_up, preferred_element_type=jnp.float32)
    shared_hidden = gelu_value(shared_pre).astype(jnp.bfloat16)
    shared_result = jnp.dot(shared_hidden, shared_down, preferred_element_type=jnp.float32)
    layer_out = (routed_out + shared_result).astype(jnp.bfloat16)
    shared_back = jnp.dot(grad_out, shared_down.T, preferred_element_type=jnp.float32)
    shared_slopes = (shared_back * gelu_slope(shared_pre)).astype(jnp.bfloat16)
    shared_grad = jnp.dot(shared_slopes, shared_up.T, preferred_element_type=jnp.float32)
    grad_tokens = (routed_grad + shared_grad).astype(jnp.bfloat16)
    grad_shared_up = jnp.dot(tokens.T, shared_slopes, preferred_element_type=jnp.float32)
    grad_shared_down = jnp.dot(shared_hidden.T, grad_out, preferred_element_type=jnp.float32)
    return layer_out, grad_tokens, grad_up, grad_down, grad_shared_up, grad_shared_down
```

```python
import jax
import jax.numpy as jnp
from jax import lax
from jax.sharding import Mesh, PartitionSpec as P

half_root = 0.7071067811865476
inv_root_tau = 0.3989422804014327

AXES = ("z", "ylo", "x", "yhi", "core")
CHIPS = ("z", "ylo", "x", "yhi")


def gelu_value(values):
    return 0.5 * values * (1.0 + lax.erf(values * half_root))


def gelu_slope(values):
    return 0.5 * (1.0 + lax.erf(values * half_root)) + values * inv_root_tau * jnp.exp(
        -0.5 * values * values
    )


def dot(left, right):
    return jnp.dot(left, right, preferred_element_type=jnp.float32)


def contract_rows(left, right):
    return lax.dot_general(
        left, right, (((0,), (0,)), ((), ())), preferred_element_type=jnp.float32
    )


def contract_cols(left, right):
    return lax.dot_general(
        left, right, (((1,), (1,)), ((), ())), preferred_element_type=jnp.float32
    )


def together(*arrays):
    return lax.optimization_barrier(arrays)


def swap(values):
    return lax.ppermute(values, "core", [(0, 1), (1, 0)])


def gather_ring(values, axis):
    count = lax.axis_size(axis)
    here = lax.axis_index(axis)
    out = jnp.zeros((count,) + values.shape, values.dtype)
    zeros = (0,) * values.ndim
    for step in range(count):
        piece = values
        if step:
            piece = lax.ppermute(
                values, axis, [((i + step) % count, i) for i in range(count)]
            )
        out = lax.dynamic_update_slice(out, piece[None], (lax.rem(here + step, count),) + zeros)
    return out


def scatter_ring(values, axis):
    count = lax.axis_size(axis)
    here = lax.axis_index(axis)
    total = lax.dynamic_index_in_dim(values, here, 0, keepdims=False).astype(jnp.float32)
    for step in range(1, count):
        chunk = lax.dynamic_index_in_dim(values, lax.rem(here + step, count), 0, keepdims=False)
        got = lax.ppermute(
            chunk.astype(jnp.bfloat16), axis, [(i, (i + step) % count) for i in range(count)]
        )
        total = total + got.astype(jnp.float32)
    return total


def exchange_sum(values, axis):
    return values + lax.ppermute(values, axis, [(0, 1), (1, 0)])


def exchange(values):
    return lax.all_to_all(values, CHIPS, split_axis=0, concat_axis=0, tiled=True)


def body(tokens, expert_ids, gate_code, grad_out, up_weight, down_weight, shared_up, shared_down):
    core = lax.axis_index("core")
    z_here = lax.axis_index("z")
    rows, width = tokens.shape
    chips = lax.axis_size("z") * lax.axis_size("ylo") * lax.axis_size("x") * lax.axis_size("yhi")
    cap = 4 * rows // (2 * chips)
    slots = chips * 2 * cap

    chip_tokens = jnp.concatenate([tokens, swap(tokens)], axis=0)
    chip_grads = jnp.concatenate([grad_out, swap(grad_out)], axis=0)

    id_rows = expert_ids.T
    order = jnp.arange(rows, dtype=jnp.int32)
    earlier = order[:, None] < order[None, :]
    positions = []
    for column in range(2):
        same = (expert_ids[:, 0:1] == id_rows[column : column + 1]) | (
            expert_ids[:, 1:2] == id_rows[column : column + 1]
        )
        positions.append(jnp.sum((same & earlier).astype(jnp.int32), axis=0))
    routes = jnp.stack(
        [id_rows[0] * cap + positions[0], id_rows[1] * cap + positions[1], gate_code]
    )
    routes_other = swap(routes)

    def targets(packed, offset):
        expert = packed[:2] // cap
        position = packed[:2] - expert * cap
        slot = (expert // 2) * (2 * cap) + offset + position
        return jnp.where(expert - (expert // 2) * 2 == core, slot, -1)

    target = jnp.concatenate([targets(routes, 0), targets(routes_other, cap)], axis=1)
    first_gate = jnp.concatenate([routes[2], routes_other[2]]).astype(jnp.float32) / 8.0
    slot_grid = jnp.arange(slots, dtype=jnp.int32)[:, None]
    hit_first = slot_grid == target[0][None, :]
    hit_second = slot_grid == target[1][None, :]
    placing = (hit_first | hit_second).astype(jnp.bfloat16)
    weighing = (
        jnp.where(hit_first, first_gate[None, :], 0.0)
        + jnp.where(hit_second, 1.0 - first_gate[None, :], 0.0)
    ).astype(jnp.bfloat16)


    hidden_rows = shared_down.shape[0]
    groups = shared_up.shape[1] // (2 * hidden_rows)
    by_core = shared_up.reshape(rows_of(shared_up), groups, 2, hidden_rows)
    up_keep = lax.dynamic_index_in_dim(by_core, core, 2, keepdims=False)
    up_send = lax.dynamic_index_in_dim(by_core, 1 - core, 2, keepdims=False)
    half = groups * hidden_rows
    up_keep = up_keep.reshape(rows_of(shared_up), half)
    up_got = swap(up_send.reshape(rows_of(shared_up), half))
    up_chip = jnp.where(
        core == 0,
        jnp.concatenate([up_keep, up_got], axis=0),
        jnp.concatenate([up_got, up_keep], axis=0),
    )
    quarters = lax.axis_size("z")
    piece = lax.dynamic_index_in_dim(
        shared_down.reshape(quarters, hidden_rows // quarters, width), z_here, 0, keepdims=False
    )
    payload = dot(placing, chip_tokens).astype(jnp.bfloat16)
    payload, up_chip, piece = together(payload, up_chip, piece)
    arrived = exchange(payload)
    up_pair = gather_ring(up_chip, "yhi")
    piece = gather_ring(piece, "yhi")
    chip_grads, up_pair, piece = together(chip_grads, up_pair, piece)
    upstream = exchange(dot(weighing, chip_grads).astype(jnp.bfloat16))
    shared_in = gather_ring(up_pair, "x").reshape(width, half)
    piece = gather_ring(piece, "x").reshape(groups, hidden_rows // quarters, width)
    shared_back_out = jnp.swapaxes(gather_ring(piece, "z"), 0, 1).reshape(half, width)
    arrived, shared_in, shared_back_out = together(arrived, shared_in, shared_back_out)

    shared_pre = dot(chip_tokens, shared_in)
    shared_hidden = gelu_value(shared_pre).astype(jnp.bfloat16)
    shared_back = contract_cols(chip_grads, shared_back_out)
    shared_slopes = (shared_back * gelu_slope(shared_pre)).astype(jnp.bfloat16)
    term_in = contract_rows(chip_tokens, shared_slopes).astype(jnp.bfloat16)
    term_out = contract_rows(shared_hidden, chip_grads).astype(jnp.bfloat16)
    shared_result = dot(shared_hidden, shared_back_out)
    shared_grad = contract_cols(shared_slopes, shared_in)

    x_count, yhi_count = lax.axis_size("x"), lax.axis_size("yhi")
    part_in = scatter_ring(term_in.reshape(x_count, -1, half), "x")
    term_out = jnp.swapaxes(term_out.reshape(groups, quarters, -1, width), 0, 1)
    part_out = scatter_ring(term_out, "z")

    upward = up_weight[0]
    downward = down_weight[0]
    preact = dot(arrived, upward)
    hidden = gelu_value(preact).astype(jnp.bfloat16)
    produced = dot(hidden, downward).astype(jnp.bfloat16)
    returned = exchange(produced)
    upstream, part_in, part_out = together(upstream, part_in, part_out)
    hidden_grad = contract_cols(upstream, downward)
    slopes = (hidden_grad * gelu_slope(preact)).astype(jnp.bfloat16)
    inward = contract_cols(slopes, upward).astype(jnp.bfloat16)
    landed = exchange(inward)
    grad_lower = contract_rows(hidden, upstream).astype(jnp.bfloat16)
    grad_upper = contract_rows(arrived, slopes).astype(jnp.bfloat16)

    part_in = scatter_ring(part_in.reshape(yhi_count, -1, half), "yhi")
    part_in = scatter_ring(part_in.reshape(quarters, -1, half), "z")
    part_in = exchange_sum(part_in, "ylo")
    part_in = gather_ring(part_in, "z").reshape(2, -1, half)
    in_keep = lax.dynamic_index_in_dim(part_in, core, 0, keepdims=False)
    in_got = swap(lax.dynamic_index_in_dim(part_in, 1 - core, 0, keepdims=False))
    in_keep = in_keep.reshape(-1, groups, hidden_rows)
    in_got = in_got.reshape(-1, groups, hidden_rows)
    sum_in = jnp.where(
        core == 0, jnp.stack([in_keep, in_got], axis=2), jnp.stack([in_got, in_keep], axis=2)
    ).reshape(shared_up.shape)
    part_out = scatter_ring(part_out.reshape(x_count, yhi_count, -1, width), "x")
    part_out = scatter_ring(part_out, "yhi")
    part_out = exchange_sum(part_out, "ylo")
    sum_out = gather_ring(part_out, "z").reshape(shared_down.shape)

    out_part = contract_rows(weighing, returned) + shared_result
    layer_out = (out_part[:rows] + swap(out_part[rows:])).astype(jnp.bfloat16)
    grad_part = contract_rows(placing, landed) + shared_grad
    grad_tokens = (grad_part[:rows] + swap(grad_part[rows:])).astype(jnp.bfloat16)
    return (layer_out, grad_tokens, grad_upper[None], grad_lower[None], sum_in, sum_out)


def rows_of(array):
    return array.shape[0]


def solution(mesh):
    node, local = mesh.shape["node"], mesh.shape["local"]
    fine = Mesh(mesh.devices.reshape(node // 2, 2, local // 4, 2, 2), AXES)
    every = AXES
    shared = ("x", "yhi", "core")
    return jax.shard_map(
        body,
        mesh=fine,
        in_specs=(
            P(every, None),
            P(every, None),
            P(every),
            P(every, None),
            P(every, None, None),
            P(every, None, None),
            P(shared, None),
            P(shared, None),
        ),
        out_specs=(
            P(every, None),
            P(every, None),
            P(every, None, None),
            P(every, None, None),
            P(shared, None),
            P(shared, None),
        ),
        check_vma=False,
    )
```

```python
import jax
import jax.numpy as jnp
from jax import lax
from jax.sharding import Mesh, PartitionSpec as P

half_root = 0.7071067811865476
inv_root_tau = 0.3989422804014327

AXES = ("z", "ylo", "x", "yhi", "core")
CHIPS = ("z", "ylo", "x", "yhi")


def gelu_value(values):
    return 0.5 * values * (1.0 + lax.erf(values * half_root))


def gelu_slope(values):
    return 0.5 * (1.0 + lax.erf(values * half_root)) + values * inv_root_tau * jnp.exp(
        -0.5 * values * values
    )


def dot(left, right):
    return jnp.dot(left, right, preferred_element_type=jnp.float32)


def contract_rows(left, right):
    return lax.dot_general(
        left, right, (((0,), (0,)), ((), ())), preferred_element_type=jnp.float32
    )


def contract_cols(left, right):
    return lax.dot_general(
        left, right, (((1,), (1,)), ((), ())), preferred_element_type=jnp.float32
    )


def together(*arrays):
    return lax.optimization_barrier(arrays)


def swap(values):
    return lax.ppermute(values, "core", [(0, 1), (1, 0)])


def place_of(axes):
    place = 0
    for axis in axes:
        place = place * lax.axis_size(axis) + lax.axis_index(axis)
    return place


def count_of(axes):
    count = 1
    for axis in axes:
        count *= lax.axis_size(axis)
    return count


def gather(values, axes):
    count = count_of(axes)
    here = place_of(axes)
    out = jnp.zeros((count,) + values.shape, values.dtype)
    zeros = (0,) * values.ndim
    for step in range(count):
        piece = values
        if step:
            piece = lax.ppermute(values, axes, [((i + step) % count, i) for i in range(count)])
        out = lax.dynamic_update_slice(out, piece[None], (lax.rem(here + step, count),) + zeros)
    return out


def scatter_sum(values, axes):
    count = count_of(axes)
    here = place_of(axes)
    total = lax.dynamic_index_in_dim(values, here, 0, keepdims=False).astype(jnp.float32)
    for step in range(1, count):
        chunk = lax.dynamic_index_in_dim(values, lax.rem(here + step, count), 0, keepdims=False)
        got = lax.ppermute(
            chunk.astype(jnp.bfloat16), axes, [(i, (i + step) % count) for i in range(count)]
        )
        total = total + got.astype(jnp.float32)
    return total


def chunks_for(values, axes, kinds):
    count = count_of(axes)
    here = place_of(axes)
    out = jnp.zeros((count,) + values.shape[1:], values.dtype)
    zeros = (0,) * (values.ndim - 1)
    for step in range(count):
        target = lax.rem(here + step, count)
        piece = lax.dynamic_index_in_dim(values, lax.rem(target, kinds), 0, keepdims=False)
        if step:
            piece = lax.ppermute(piece, axes, [(i, (i + step) % count) for i in range(count)])
        origin = lax.rem(here + count - step, count)
        out = lax.dynamic_update_slice(out, piece[None], (origin,) + zeros)
    return out


def exchange(values):
    return lax.all_to_all(values, CHIPS, split_axis=0, concat_axis=0, tiled=True)


def body(tokens, expert_ids, gate_code, grad_out, up_weight, down_weight, shared_up, shared_down):
    core = lax.axis_index("core")
    z_here = lax.axis_index("z")
    rows, width = tokens.shape
    chips = lax.axis_size("z") * lax.axis_size("ylo") * lax.axis_size("x") * lax.axis_size("yhi")
    cap = 4 * rows // (2 * chips)
    slots = chips * 2 * cap

    chip_tokens = jnp.concatenate([tokens, swap(tokens)], axis=0)
    chip_grads = jnp.concatenate([grad_out, swap(grad_out)], axis=0)

    id_rows = expert_ids.T
    order = jnp.arange(rows, dtype=jnp.int32)
    earlier = order[:, None] < order[None, :]
    positions = []
    for column in range(2):
        same = (expert_ids[:, 0:1] == id_rows[column : column + 1]) | (
            expert_ids[:, 1:2] == id_rows[column : column + 1]
        )
        positions.append(jnp.sum((same & earlier).astype(jnp.int32), axis=0))
    routes = jnp.stack(
        [id_rows[0] * cap + positions[0], id_rows[1] * cap + positions[1], gate_code]
    )
    routes_other = swap(routes)

    def targets(packed, offset):
        expert = packed[:2] // cap
        position = packed[:2] - expert * cap
        slot = (expert // 2) * (2 * cap) + offset + position
        return jnp.where(expert - (expert // 2) * 2 == core, slot, -1)

    target = jnp.concatenate([targets(routes, 0), targets(routes_other, cap)], axis=1)
    first_gate = jnp.concatenate([routes[2], routes_other[2]]).astype(jnp.float32) / 8.0
    slot_grid = jnp.arange(slots, dtype=jnp.int32)[:, None]
    hit_first = slot_grid == target[0][None, :]
    hit_second = slot_grid == target[1][None, :]
    placing = (hit_first | hit_second).astype(jnp.bfloat16)
    weighing = (
        jnp.where(hit_first, first_gate[None, :], 0.0)
        + jnp.where(hit_second, 1.0 - first_gate[None, :], 0.0)
    ).astype(jnp.bfloat16)


    hidden_rows = shared_down.shape[0]
    groups = shared_up.shape[1] // (2 * hidden_rows)
    by_core = shared_up.reshape(rows_of(shared_up), groups, 2, hidden_rows)
    up_keep = lax.dynamic_index_in_dim(by_core, core, 2, keepdims=False)
    up_send = lax.dynamic_index_in_dim(by_core, 1 - core, 2, keepdims=False)
    half = groups * hidden_rows
    up_keep = up_keep.reshape(rows_of(shared_up), half)
    up_got = swap(up_send.reshape(rows_of(shared_up), half))
    up_chip = jnp.where(
        core == 0,
        jnp.concatenate([up_keep, up_got], axis=0),
        jnp.concatenate([up_got, up_keep], axis=0),
    )
    quarters = lax.axis_size("z")
    piece = lax.dynamic_index_in_dim(
        shared_down.reshape(quarters, hidden_rows // quarters, width), z_here, 0, keepdims=False
    )
    piece = gather(gather(piece, ("yhi",)), ("x",)).reshape(groups, -1, width)
    up_pair = gather(up_chip, ("yhi",))
    payload = dot(placing, chip_tokens).astype(jnp.bfloat16)
    payload, up_pair, piece = together(payload, up_pair, piece)
    arrived = exchange(payload)
    upstream = exchange(dot(weighing, chip_grads).astype(jnp.bfloat16))
    shared_in = gather(up_pair, ("x",)).reshape(width, half)
    shared_back_out = jnp.swapaxes(gather(piece, ("z",)), 0, 1).reshape(half, width)
    arrived, shared_in, shared_back_out = together(arrived, shared_in, shared_back_out)

    shared_pre = dot(chip_tokens, shared_in)
    shared_hidden = gelu_value(shared_pre).astype(jnp.bfloat16)
    shared_back = contract_cols(chip_grads, shared_back_out)
    shared_slopes = (shared_back * gelu_slope(shared_pre)).astype(jnp.bfloat16)
    term_in = contract_rows(chip_tokens, shared_slopes).astype(jnp.bfloat16)
    term_out = contract_rows(shared_hidden, chip_grads).astype(jnp.bfloat16)

    x_count, yhi_count = lax.axis_size("x"), lax.axis_size("yhi")
    part_in = scatter_sum(term_in.reshape(x_count, -1, half), ("x",))
    term_out = jnp.swapaxes(term_out.reshape(groups, quarters, -1, width), 0, 1)
    part_out = scatter_sum(term_out, ("z",))

    upward = up_weight[0]
    downward = down_weight[0]
    preact = dot(arrived, upward)
    hidden = gelu_value(preact).astype(jnp.bfloat16)
    produced = dot(hidden, downward).astype(jnp.bfloat16)
    returned = exchange(produced)
    upstream, part_in, part_out = together(upstream, part_in, part_out)
    hidden_grad = contract_cols(upstream, downward)
    slopes = (hidden_grad * gelu_slope(preact)).astype(jnp.bfloat16)
    inward = contract_cols(slopes, upward).astype(jnp.bfloat16)
    landed = exchange(inward)

    part_in = part_in.reshape(yhi_count, 2, quarters, -1, half).transpose(2, 0, 1, 3, 4)
    part_in = scatter_sum(part_in, ("z",)).reshape(yhi_count, -1, half)
    part_out = scatter_sum(part_out.reshape(x_count, yhi_count, -1, width), ("x",))
    part = jnp.stack([part_in, part_out.reshape(part_in.shape)], axis=1).astype(jnp.bfloat16)
    returned, slopes, part = together(returned, slopes, part)

    def combine(routing, rows_back, shared_left, shared_right):
        far = contract_rows(routing[:, rows:], rows_back) + shared_right(shared_left[rows:])
        far = swap(far.astype(jnp.bfloat16))
        near = contract_rows(routing[:, :rows], rows_back) + shared_right(shared_left[:rows])
        return (near + far.astype(jnp.float32)).astype(jnp.bfloat16)

    layer_out = combine(weighing, returned, shared_hidden, lambda left: dot(left, shared_back_out))
    grad_upper = contract_rows(arrived, slopes).astype(jnp.bfloat16)
    grad_lower = contract_rows(hidden, upstream).astype(jnp.bfloat16)

    along_y = ("ylo", "yhi")
    parts = chunks_for(part, along_y, yhi_count).astype(jnp.float32).sum(axis=0)
    sum_in = parts[0].reshape(2, -1, half)
    in_keep = lax.dynamic_index_in_dim(sum_in, core, 0, keepdims=False)
    in_got = swap(lax.dynamic_index_in_dim(sum_in, 1 - core, 0, keepdims=False))
    in_keep = in_keep.reshape(-1, groups, hidden_rows)
    in_got = in_got.reshape(-1, groups, hidden_rows)
    sum_in = jnp.where(
        core == 0, jnp.stack([in_keep, in_got], axis=2), jnp.stack([in_got, in_keep], axis=2)
    ).reshape(-1, shared_up.shape[1])
    sum_out = parts[1].reshape(sum_in.shape)

    sums = gather(jnp.stack([sum_in, sum_out]).astype(jnp.bfloat16), ("z",)).astype(jnp.float32)
    sum_in = sums[:, 0].reshape(shared_up.shape)
    sum_out = sums[:, 1].reshape(shared_down.shape)

    grad_tokens = combine(placing, landed, shared_slopes, lambda left: contract_cols(left, shared_in))
    return (layer_out, grad_tokens, grad_upper[None], grad_lower[None], sum_in, sum_out)


def rows_of(array):
    return array.shape[0]


def solution(mesh):
    node, local = mesh.shape["node"], mesh.shape["local"]
    fine = Mesh(mesh.devices.reshape(node // 2, 2, local // 4, 2, 2), AXES)
    every = AXES
    shared = ("x", "yhi", "core")
    return jax.shard_map(
        body,
        mesh=fine,
        in_specs=(
            P(every, None),
            P(every, None),
            P(every),
            P(every, None),
            P(every, None, None),
            P(every, None, None),
            P(shared, None),
            P(shared, None),
        ),
        out_specs=(
            P(every, None),
            P(every, None),
            P(every, None, None),
            P(every, None, None),
            P(shared, None),
            P(shared, None),
        ),
        check_vma=False,
    )
```

```python
import jax
import jax.numpy as jnp
from jax import lax
from jax.sharding import Mesh, PartitionSpec as P

half_root = 0.7071067811865476
inv_root_tau = 0.3989422804014327

AXES = ("z", "ylo", "x", "yhi", "core")
CHIPS = ("z", "ylo", "x", "yhi")


def gelu_value(values):
    return 0.5 * values * (1.0 + lax.erf(values * half_root))


def gelu_slope(values):
    return 0.5 * (1.0 + lax.erf(values * half_root)) + values * inv_root_tau * jnp.exp(
        -0.5 * values * values
    )


def dot(left, right):
    return jnp.dot(left, right, preferred_element_type=jnp.float32)


def contract_rows(left, right):
    return lax.dot_general(
        left, right, (((0,), (0,)), ((), ())), preferred_element_type=jnp.float32
    )


def contract_cols(left, right):
    return lax.dot_general(
        left, right, (((1,), (1,)), ((), ())), preferred_element_type=jnp.float32
    )


def together(*arrays):
    return lax.optimization_barrier(arrays)


def swap(values):
    return lax.ppermute(values, "core", [(0, 1), (1, 0)])


def place_of(axes):
    place = 0
    for axis in axes:
        place = place * lax.axis_size(axis) + lax.axis_index(axis)
    return place


def count_of(axes):
    count = 1
    for axis in axes:
        count *= lax.axis_size(axis)
    return count


def collect(values, axes):
    count = count_of(axes)
    return jnp.stack(
        [values]
        + [
            lax.ppermute(values, axes, [((i + step) % count, i) for i in range(count)])
            for step in range(1, count)
        ]
    )


def in_order(stacked, axes, dim=0):
    count = count_of(axes)
    here = place_of(axes)
    out = jnp.zeros_like(stacked)
    for step in range(count):
        at = [0] * stacked.ndim
        at[dim] = lax.rem(here + step, count)
        out = lax.dynamic_update_slice(
            out, lax.slice_in_dim(stacked, step, step + 1, axis=dim), tuple(at)
        )
    return out


def gather(values, axes):
    return in_order(collect(values, axes), axes)


def scatter_sum(values, axes):
    count = count_of(axes)
    here = place_of(axes)
    total = lax.dynamic_index_in_dim(values, here, 0, keepdims=False).astype(jnp.float32)
    for step in range(1, count):
        chunk = lax.dynamic_index_in_dim(values, lax.rem(here + step, count), 0, keepdims=False)
        got = lax.ppermute(
            chunk.astype(jnp.bfloat16), axes, [(i, (i + step) % count) for i in range(count)]
        )
        total = total + got.astype(jnp.float32)
    return total


def chunks_for(values, axes, kinds):
    count = count_of(axes)
    here = place_of(axes)
    out = jnp.zeros((count,) + values.shape[1:], values.dtype)
    zeros = (0,) * (values.ndim - 1)
    for step in range(count):
        target = lax.rem(here + step, count)
        piece = lax.dynamic_index_in_dim(values, lax.rem(target, kinds), 0, keepdims=False)
        if step:
            piece = lax.ppermute(piece, axes, [(i, (i + step) % count) for i in range(count)])
        origin = lax.rem(here + count - step, count)
        out = lax.dynamic_update_slice(out, piece[None], (origin,) + zeros)
    return out


def exchange(values):
    return lax.all_to_all(values, CHIPS, split_axis=0, concat_axis=0, tiled=True)


def body(tokens, expert_ids, gate_code, grad_out, up_weight, down_weight, shared_up, shared_down):
    core = lax.axis_index("core")
    z_here = lax.axis_index("z")
    rows, width = tokens.shape
    chips = lax.axis_size("z") * lax.axis_size("ylo") * lax.axis_size("x") * lax.axis_size("yhi")
    cap = 4 * rows // (2 * chips)
    slots = chips * 2 * cap

    chip_tokens = jnp.concatenate([tokens, swap(tokens)], axis=0)
    chip_grads = jnp.concatenate([grad_out, swap(grad_out)], axis=0)

    id_rows = expert_ids.T
    order = jnp.arange(rows, dtype=jnp.int32)
    earlier = order[:, None] < order[None, :]
    positions = []
    for column in range(2):
        same = (expert_ids[:, 0:1] == id_rows[column : column + 1]) | (
            expert_ids[:, 1:2] == id_rows[column : column + 1]
        )
        positions.append(jnp.sum((same & earlier).astype(jnp.int32), axis=0))
    routes = jnp.stack(
        [id_rows[0] * cap + positions[0], id_rows[1] * cap + positions[1], gate_code]
    )
    routes_other = swap(routes)

    def targets(packed, offset):
        expert = packed[:2] // cap
        position = packed[:2] - expert * cap
        slot = (expert // 2) * (2 * cap) + offset + position
        return jnp.where(expert - (expert // 2) * 2 == core, slot, -1)

    target = jnp.concatenate([targets(routes, 0), targets(routes_other, cap)], axis=1)
    first_gate = jnp.concatenate([routes[2], routes_other[2]]).astype(jnp.float32) / 8.0
    slot_grid = jnp.arange(slots, dtype=jnp.int32)[:, None]
    hit_first = slot_grid == target[0][None, :]
    hit_second = slot_grid == target[1][None, :]
    placing = (hit_first | hit_second).astype(jnp.bfloat16)
    weighing = (
        jnp.where(hit_first, first_gate[None, :], 0.0)
        + jnp.where(hit_second, 1.0 - first_gate[None, :], 0.0)
    ).astype(jnp.bfloat16)


    hidden_rows = shared_down.shape[0]
    groups = shared_up.shape[1] // (2 * hidden_rows)
    half = groups * hidden_rows
    unit = jnp.arange(2 * half, dtype=jnp.int32)
    picked = lax.rem(unit, half)
    side = jnp.where(unit < half, core, 1 - core)
    picked = (picked // hidden_rows) * (2 * hidden_rows) + side * hidden_rows + picked % hidden_rows
    picking = (unit[:, None] == picked[None, :]).astype(jnp.bfloat16)
    by_core = dot(shared_up, picking).astype(jnp.bfloat16)
    up_keep, up_got = by_core[:, :half], swap(by_core[:, half:])
    up_chip = jnp.where(
        core == 0,
        jnp.concatenate([up_keep, up_got], axis=0),
        jnp.concatenate([up_got, up_keep], axis=0),
    )
    quarters, x_count, yhi_count = lax.axis_size("z"), lax.axis_size("x"), lax.axis_size("yhi")
    piece = lax.dynamic_index_in_dim(
        shared_down.reshape(quarters, hidden_rows // quarters, width), z_here, 0, keepdims=False
    )
    piece = collect(collect(piece, ("yhi",)), ("x",))
    up_pair = collect(up_chip, ("yhi",))
    payload = jnp.concatenate(
        [
            dot(placing, chip_tokens).astype(jnp.bfloat16),
            dot(weighing, chip_grads).astype(jnp.bfloat16),
        ],
        axis=1,
    )
    payload, up_pair, piece = together(payload, up_pair, piece)
    arrived_both = exchange(payload)
    shared_in = in_order(gather(up_pair, ("x",)), ("yhi",), 1).reshape(width, half)
    piece = in_order(in_order(collect(piece, ("z",)), ("yhi",), 2), ("x",), 1)
    piece = in_order(piece, ("z",)).reshape(quarters, groups, -1, width)
    shared_back_out = jnp.swapaxes(piece, 0, 1).reshape(half, width)

    shared_pre = dot(chip_tokens, shared_in)
    shared_hidden = gelu_value(shared_pre).astype(jnp.bfloat16)
    shared_back = contract_cols(chip_grads, shared_back_out)
    shared_slopes = (shared_back * gelu_slope(shared_pre)).astype(jnp.bfloat16)
    term_in = contract_rows(chip_tokens, shared_slopes).astype(jnp.bfloat16)
    term_out = contract_rows(shared_hidden, chip_grads).astype(jnp.bfloat16)

    part_in = scatter_sum(term_in.reshape(x_count, -1, half), ("x",))
    term_out = jnp.swapaxes(term_out.reshape(groups, quarters, -1, width), 0, 1)
    part_out = scatter_sum(term_out, ("z",))
    arrived_both, part_in, part_out = together(arrived_both, part_in, part_out)

    upward = up_weight[0]
    downward = down_weight[0]
    arrived, upstream = arrived_both[:, :width], arrived_both[:, width:]
    preact = dot(arrived, upward)
    hidden = gelu_value(preact).astype(jnp.bfloat16)
    produced = dot(hidden, downward).astype(jnp.bfloat16)
    hidden_grad = contract_cols(upstream, downward)
    slopes = (hidden_grad * gelu_slope(preact)).astype(jnp.bfloat16)
    inward = contract_cols(slopes, upward).astype(jnp.bfloat16)
    landed_both = exchange(jnp.concatenate([produced, inward], axis=1))

    part_in = part_in.reshape(yhi_count, 2, quarters, -1, half).transpose(2, 0, 1, 3, 4)
    part_in = scatter_sum(part_in, ("z",)).reshape(yhi_count, -1, half)
    part_out = scatter_sum(part_out.reshape(x_count, yhi_count, -1, width), ("x",))
    part = jnp.stack([part_in, part_out.reshape(part_in.shape)], axis=1).astype(jnp.bfloat16)
    grad_upper = contract_rows(arrived, slopes).astype(jnp.bfloat16)
    grad_lower = contract_rows(hidden, upstream).astype(jnp.bfloat16)

    def combine(routing, rows_back, shared_left, shared_right):
        far = contract_rows(routing[:, rows:], rows_back) + shared_right(shared_left[rows:])
        far = swap(far.astype(jnp.bfloat16))
        near = contract_rows(routing[:, :rows], rows_back) + shared_right(shared_left[:rows])
        return (near + far.astype(jnp.float32)).astype(jnp.bfloat16)

    along_y = ("ylo", "yhi")
    parts = chunks_for(part, along_y, yhi_count).astype(jnp.float32).sum(axis=0)
    sum_in = parts[0].reshape(2, -1, half)
    in_keep = lax.dynamic_index_in_dim(sum_in, core, 0, keepdims=False)
    in_got = swap(lax.dynamic_index_in_dim(sum_in, 1 - core, 0, keepdims=False))
    in_keep = in_keep.reshape(-1, groups, hidden_rows)
    in_got = in_got.reshape(-1, groups, hidden_rows)
    sum_in = jnp.where(
        core == 0, jnp.stack([in_keep, in_got], axis=2), jnp.stack([in_got, in_keep], axis=2)
    ).reshape(-1, shared_up.shape[1])
    sum_out = parts[1].reshape(sum_in.shape)

    sums = gather(jnp.stack([sum_in, sum_out]).astype(jnp.bfloat16), ("z",)).astype(jnp.float32)
    sum_in = sums[:, 0].reshape(shared_up.shape)
    sum_out = sums[:, 1].reshape(shared_down.shape)

    returned, landed = landed_both[:, :width], landed_both[:, width:]
    layer_out = combine(weighing, returned, shared_hidden, lambda left: dot(left, shared_back_out))
    grad_tokens = combine(placing, landed, shared_slopes, lambda left: contract_cols(left, shared_in))
    return (layer_out, grad_tokens, grad_upper[None], grad_lower[None], sum_in, sum_out)


def rows_of(array):
    return array.shape[0]


def solution(mesh):
    node, local = mesh.shape["node"], mesh.shape["local"]
    fine = Mesh(mesh.devices.reshape(node // 2, 2, local // 4, 2, 2), AXES)
    every = AXES
    shared = ("x", "yhi", "core")
    return jax.shard_map(
        body,
        mesh=fine,
        in_specs=(
            P(every, None),
            P(every, None),
            P(every),
            P(every, None),
            P(every, None, None),
            P(every, None, None),
            P(shared, None),
            P(shared, None),
        ),
        out_specs=(
            P(every, None),
            P(every, None),
            P(every, None, None),
            P(every, None, None),
            P(shared, None),
            P(shared, None),
        ),
        check_vma=False,
    )
```

```python
import jax
import jax.numpy as jnp
from jax import lax
from jax.sharding import Mesh, PartitionSpec as P

half_root = 0.7071067811865476
inv_root_tau = 0.3989422804014327

AXES = ("z", "ylo", "x", "yhi", "core")
CHIPS = ("z", "ylo", "x", "yhi")
LOCAL = ("x", "yhi")
NODE = ("z", "ylo")


def gelu_value(values):
    return 0.5 * values * (1.0 + lax.erf(values * half_root))


def gelu_slope(values):
    return 0.5 * (1.0 + lax.erf(values * half_root)) + values * inv_root_tau * jnp.exp(
        -0.5 * values * values
    )


def dot(left, right):
    return jnp.dot(left, right, preferred_element_type=jnp.float32)


def contract_rows(left, right):
    return lax.dot_general(
        left, right, (((0,), (0,)), ((), ())), preferred_element_type=jnp.float32
    )


def contract_cols(left, right):
    return lax.dot_general(
        left, right, (((1,), (1,)), ((), ())), preferred_element_type=jnp.float32
    )


def together(*arrays):
    return lax.optimization_barrier(arrays)


def swap(values):
    return lax.ppermute(values, "core", [(0, 1), (1, 0)])


def exchange(values):
    return lax.all_to_all(values, CHIPS, split_axis=0, concat_axis=0, tiled=True)


def body(tokens, expert_ids, gate_code, grad_out, up_weight, down_weight, shared_up, shared_down):
    core = lax.axis_index("core")
    rows, width = tokens.shape
    chips = lax.axis_size("z") * lax.axis_size("ylo") * lax.axis_size("x") * lax.axis_size("yhi")
    cap = 4 * rows // (2 * chips)
    slots = chips * 2 * cap

    chip_tokens = jnp.concatenate([tokens, swap(tokens)], axis=0)
    chip_grads = jnp.concatenate([grad_out, swap(grad_out)], axis=0)

    id_rows = expert_ids.T
    order = jnp.arange(rows, dtype=jnp.int32)
    earlier = order[:, None] < order[None, :]
    positions = []
    for column in range(2):
        same = (expert_ids[:, 0:1] == id_rows[column : column + 1]) | (
            expert_ids[:, 1:2] == id_rows[column : column + 1]
        )
        positions.append(jnp.sum((same & earlier).astype(jnp.int32), axis=0))
    routes = jnp.stack(
        [id_rows[0] * cap + positions[0], id_rows[1] * cap + positions[1], gate_code]
    )
    routes_other = swap(routes)

    def targets(packed, offset):
        expert = packed[:2] // cap
        position = packed[:2] - expert * cap
        slot = (expert // 2) * (2 * cap) + offset + position
        return jnp.where(expert - (expert // 2) * 2 == core, slot, -1)

    target = jnp.concatenate([targets(routes, 0), targets(routes_other, cap)], axis=1)
    first_gate = jnp.concatenate([routes[2], routes_other[2]]).astype(jnp.float32) / 8.0
    slot_grid = jnp.arange(slots, dtype=jnp.int32)[:, None]
    hit_first = slot_grid == target[0][None, :]
    hit_second = slot_grid == target[1][None, :]
    placing = (hit_first | hit_second).astype(jnp.bfloat16)
    weighing = (
        jnp.where(hit_first, first_gate[None, :], 0.0)
        + jnp.where(hit_second, 1.0 - first_gate[None, :], 0.0)
    ).astype(jnp.bfloat16)


    hidden_rows = shared_down.shape[0]
    groups = shared_up.shape[1] // (2 * hidden_rows)
    nodes = lax.axis_size("z") * lax.axis_size("ylo")
    few = hidden_rows // nodes
    half = groups * hidden_rows
    unit = jnp.arange(2 * half, dtype=jnp.int32)
    inner = lax.rem(unit, half)
    side = jnp.where(unit < half, core, 1 - core)
    picked = (lax.rem(inner // few, groups) * 2 + side) * hidden_rows
    picked = picked + (inner // (groups * few)) * few + lax.rem(inner, few)
    picking = (unit[:, None] == picked[None, :]).astype(jnp.bfloat16)
    by_core = dot(shared_up, picking).astype(jnp.bfloat16)
    up_keep, up_got = by_core[:, :half], swap(by_core[:, half:])
    up_chip = jnp.where(
        core == 0,
        jnp.concatenate([up_keep, up_got], axis=0),
        jnp.concatenate([up_got, up_keep], axis=0),
    )
    shared_in = lax.all_gather(up_chip, LOCAL, axis=0, tiled=True)
    payload = dot(placing, chip_tokens).astype(jnp.bfloat16)
    payload, chip_grads, shared_down = together(payload, chip_grads, shared_down)
    shared_back_out = lax.all_gather(shared_down, LOCAL, axis=0, tiled=True)
    shared_back_out = shared_back_out.reshape(groups, nodes, few, width)
    shared_back_out = shared_back_out.transpose(1, 0, 2, 3).reshape(half, width)
    arrived = exchange(payload)
    upstream = exchange(dot(weighing, chip_grads).astype(jnp.bfloat16))

    shared_pre = dot(chip_tokens, shared_in)
    shared_hidden = gelu_value(shared_pre).astype(jnp.bfloat16)
    term_out = contract_rows(shared_hidden, chip_grads).astype(jnp.bfloat16)
    upward = up_weight[0]
    downward = down_weight[0]
    preact = dot(arrived, upward)
    hidden = gelu_value(preact).astype(jnp.bfloat16)
    produced = dot(hidden, downward).astype(jnp.bfloat16)
    back = jnp.concatenate([produced, term_out], axis=1)
    back, upstream, shared_pre = together(back, upstream, shared_pre)
    returned = exchange(back)

    hidden_grad = contract_cols(upstream, downward)
    slopes = (hidden_grad * gelu_slope(preact)).astype(jnp.bfloat16)
    inward = contract_cols(slopes, upward).astype(jnp.bfloat16)
    shared_back = contract_cols(chip_grads, shared_back_out)
    shared_slopes = (shared_back * gelu_slope(shared_pre)).astype(jnp.bfloat16)
    term_in = contract_rows(chip_tokens, shared_slopes).astype(jnp.bfloat16)
    slab = width // (groups * nodes)
    term_in = term_in.reshape(groups, nodes, slab // few, few, half).transpose(1, 0, 3, 2, 4)
    landed = exchange(jnp.concatenate([inward, term_in.reshape(half, width)], axis=1))

    def total(parts):
        parts = parts.reshape(chips, few, width).astype(jnp.float32)
        return parts.sum(axis=0).astype(jnp.bfloat16)

    def parts_of(routing, rows_back, shared_part):
        near = contract_rows(routing[:, :rows], rows_back) + shared_part[:rows]
        far = contract_rows(routing[:, rows:], rows_back) + shared_part[rows:]
        return near, far.astype(jnp.bfloat16)

    def whole(near, far):
        return (near + swap(far).astype(jnp.float32)).astype(jnp.bfloat16)

    out_near, out_far = parts_of(weighing, returned[:, :width], dot(shared_hidden, shared_back_out))
    shared_grad = contract_cols(shared_slopes, shared_in)
    total_out = total(returned[:, width:])
    out_near, out_far, shared_grad, total_out, slopes = together(
        out_near, out_far, shared_grad, total_out, slopes
    )
    grad_upper = contract_rows(arrived, slopes).astype(jnp.bfloat16)
    grad_lower = contract_rows(hidden, upstream).astype(jnp.bfloat16)

    grad_near, grad_far = parts_of(placing, landed[:, :width], shared_grad)
    totals = jnp.concatenate([total_out, total(landed[:, width:])], axis=1)
    layer_out = whole(out_near, out_far)
    grad_tokens = whole(grad_near, grad_far)
    totals = lax.all_gather(totals, NODE, axis=0, tiled=True)
    sum_out = totals[:, :width].astype(jnp.float32)
    sum_in = totals[:, width:].reshape(nodes, few, slab // few, half).swapaxes(1, 2)
    sum_in = sum_in.reshape(2, -1, half)
    in_keep = lax.dynamic_index_in_dim(sum_in, core, 0, keepdims=False)
    in_got = swap(lax.dynamic_index_in_dim(sum_in, 1 - core, 0, keepdims=False))
    sum_in = contract_cols(jnp.concatenate([in_keep, in_got], axis=1), picking)
    return (layer_out, grad_tokens, grad_upper[None], grad_lower[None], sum_in, sum_out)


def solution(mesh):
    node, local = mesh.shape["node"], mesh.shape["local"]
    fine = Mesh(mesh.devices.reshape(node // 2, 2, local // 4, 2, 2), AXES)
    every = AXES
    shared = ("x", "yhi", "core")
    return jax.shard_map(
        body,
        mesh=fine,
        in_specs=(
            P(every, None),
            P(every, None),
            P(every),
            P(every, None),
            P(every, None, None),
            P(every, None, None),
            P(shared, None),
            P(shared, None),
        ),
        out_specs=(
            P(every, None),
            P(every, None),
            P(every, None, None),
            P(every, None, None),
            P(shared, None),
            P(shared, None),
        ),
        check_vma=False,
    )
```

```python
import jax
import jax.numpy as jnp
from jax import lax
from jax.sharding import Mesh, PartitionSpec as P

half_root = 0.7071067811865476
inv_root_tau = 0.3989422804014327

AXES = ("z", "ylo", "x", "yhi", "core")
CHIPS = ("z", "ylo", "x", "yhi")


def gelu_value(values):
    return 0.5 * values * (1.0 + lax.erf(values * half_root))


def gelu_slope(values):
    return 0.5 * (1.0 + lax.erf(values * half_root)) + values * inv_root_tau * jnp.exp(
        -0.5 * values * values
    )


def dot(left, right):
    return jnp.dot(left, right, preferred_element_type=jnp.float32)


def contract_rows(left, right):
    return lax.dot_general(
        left, right, (((0,), (0,)), ((), ())), preferred_element_type=jnp.float32
    )


def contract_cols(left, right):
    return lax.dot_general(
        left, right, (((1,), (1,)), ((), ())), preferred_element_type=jnp.float32
    )


def together(*arrays):
    return lax.optimization_barrier(arrays)


def swap(values):
    return lax.ppermute(values, "core", [(0, 1), (1, 0)])


def gather(values, axis):
    count = lax.axis_size(axis)
    here = lax.axis_index(axis)
    out = jnp.zeros((count,) + values.shape, values.dtype)
    zeros = (0,) * values.ndim
    for step in range(count):
        piece = values
        if step:
            piece = lax.ppermute(values, axis, [((i + step) % count, i) for i in range(count)])
        out = lax.dynamic_update_slice(out, piece[None], (lax.rem(here + step, count),) + zeros)
    return out


def exchange(values):
    return lax.all_to_all(values, CHIPS, split_axis=0, concat_axis=0, tiled=True)


def body(tokens, expert_ids, gate_code, grad_out, up_weight, down_weight, shared_up, shared_down):
    core = lax.axis_index("core")
    rows, width = tokens.shape
    chips = lax.axis_size("z") * lax.axis_size("ylo") * lax.axis_size("x") * lax.axis_size("yhi")
    cap = 4 * rows // (2 * chips)
    slots = chips * 2 * cap

    chip_tokens = jnp.concatenate([tokens, swap(tokens)], axis=0)
    chip_grads = jnp.concatenate([grad_out, swap(grad_out)], axis=0)

    id_rows = expert_ids.T
    order = jnp.arange(rows, dtype=jnp.int32)
    earlier = order[:, None] < order[None, :]
    positions = []
    for column in range(2):
        same = (expert_ids[:, 0:1] == id_rows[column : column + 1]) | (
            expert_ids[:, 1:2] == id_rows[column : column + 1]
        )
        positions.append(jnp.sum((same & earlier).astype(jnp.int32), axis=0))
    routes = jnp.stack(
        [id_rows[0] * cap + positions[0], id_rows[1] * cap + positions[1], gate_code]
    )
    routes_other = swap(routes)

    def targets(packed, offset):
        expert = packed[:2] // cap
        position = packed[:2] - expert * cap
        slot = (expert // 2) * (2 * cap) + offset + position
        return jnp.where(expert - (expert // 2) * 2 == core, slot, -1)

    target = jnp.concatenate([targets(routes, 0), targets(routes_other, cap)], axis=1)
    first_gate = jnp.concatenate([routes[2], routes_other[2]]).astype(jnp.float32) / 8.0
    slot_grid = jnp.arange(slots, dtype=jnp.int32)[:, None]
    hit_first = slot_grid == target[0][None, :]
    hit_second = slot_grid == target[1][None, :]
    placing = (hit_first | hit_second).astype(jnp.bfloat16)
    weighing = (
        jnp.where(hit_first, first_gate[None, :], 0.0)
        + jnp.where(hit_second, 1.0 - first_gate[None, :], 0.0)
    ).astype(jnp.bfloat16)


    hidden_rows = shared_down.shape[0]
    groups = shared_up.shape[1] // (2 * hidden_rows)
    nodes = lax.axis_size("z") * lax.axis_size("ylo")
    few = hidden_rows // nodes
    half = groups * hidden_rows
    unit = jnp.arange(2 * half, dtype=jnp.int32)
    inner = lax.rem(unit, half)
    side = jnp.where(unit < half, core, 1 - core)
    picked = (lax.rem(inner // few, groups) * 2 + side) * hidden_rows
    picked = picked + (inner // (groups * few)) * few + lax.rem(inner, few)
    picking = (unit[:, None] == picked[None, :]).astype(jnp.bfloat16)
    by_core = dot(shared_up, picking).astype(jnp.bfloat16)
    up_keep, up_got = by_core[:, :half], swap(by_core[:, half:])
    up_chip = jnp.where(
        core == 0,
        jnp.concatenate([up_keep, up_got], axis=0),
        jnp.concatenate([up_got, up_keep], axis=0),
    )
    node = lax.axis_index("z") * lax.axis_size("ylo") + lax.axis_index("ylo")
    slab = width // (groups * nodes)
    up_slab = lax.dynamic_slice_in_dim(up_chip, node * slab, slab, 0)
    up_slab = up_slab.reshape(slab // few, few, half).swapaxes(0, 1).reshape(few, width)
    down_slab = lax.dynamic_slice_in_dim(shared_down, node * few, few, 0)

    def beside(routed, slab_rows):
        copies = jnp.broadcast_to(slab_rows[None], (chips, few, width)).reshape(chips * few, width)
        return jnp.concatenate([routed, copies], axis=1)

    payload = beside(dot(placing, chip_tokens).astype(jnp.bfloat16), up_slab)
    payload, chip_grads, down_slab = together(payload, chip_grads, down_slab)
    arrived_both = exchange(payload)
    upstream_both = exchange(beside(dot(weighing, chip_grads).astype(jnp.bfloat16), down_slab))
    arrived = arrived_both[:, :width]
    shared_in = arrived_both[:, width:].reshape(nodes, groups, few, slab // few, half)
    shared_in = shared_in.transpose(1, 0, 3, 2, 4).reshape(width, half)

    shared_pre = dot(chip_tokens, shared_in)
    shared_hidden = gelu_value(shared_pre).astype(jnp.bfloat16)
    term_out = contract_rows(shared_hidden, chip_grads).astype(jnp.bfloat16)
    upward = up_weight[0]
    downward = down_weight[0]
    preact = dot(arrived, upward)
    hidden = gelu_value(preact).astype(jnp.bfloat16)
    produced = dot(hidden, downward).astype(jnp.bfloat16)
    back = jnp.concatenate([produced, term_out], axis=1)
    back, upstream_both, shared_pre = together(back, upstream_both, shared_pre)
    returned = exchange(back)
    upstream, shared_back_out = upstream_both[:, :width], upstream_both[:, width:]

    hidden_grad = contract_cols(upstream, downward)
    slopes = (hidden_grad * gelu_slope(preact)).astype(jnp.bfloat16)
    inward = contract_cols(slopes, upward).astype(jnp.bfloat16)
    shared_back = contract_cols(chip_grads, shared_back_out)
    shared_slopes = (shared_back * gelu_slope(shared_pre)).astype(jnp.bfloat16)
    term_in = contract_rows(chip_tokens, shared_slopes).astype(jnp.bfloat16)
    term_in = term_in.reshape(groups, nodes, slab // few, few, half).transpose(1, 0, 3, 2, 4)
    landed = exchange(jnp.concatenate([inward, term_in.reshape(half, width)], axis=1))

    def total(parts):
        parts = parts.reshape(chips, few, width).astype(jnp.float32)
        return parts.sum(axis=0).astype(jnp.bfloat16)

    def parts_of(routing, rows_back, shared_part):
        near = contract_rows(routing[:, :rows], rows_back) + shared_part[:rows]
        far = contract_rows(routing[:, rows:], rows_back) + shared_part[rows:]
        return near, far.astype(jnp.bfloat16)

    def whole(near, far):
        return (near + swap(far).astype(jnp.float32)).astype(jnp.bfloat16)

    out_near, out_far = parts_of(weighing, returned[:, :width], dot(shared_hidden, shared_back_out))
    shared_grad = contract_cols(shared_slopes, shared_in)
    total_out = total(returned[:, width:])
    out_near, out_far, shared_grad, total_out, slopes = together(
        out_near, out_far, shared_grad, total_out, slopes
    )
    grad_upper = contract_rows(arrived, slopes).astype(jnp.bfloat16)
    grad_lower = contract_rows(hidden, upstream).astype(jnp.bfloat16)

    landed, grad_upper, grad_lower = together(landed, grad_upper, grad_lower)
    grad_near, grad_far = parts_of(placing, landed[:, :width], shared_grad)
    totals = jnp.concatenate([total_out, total(landed[:, width:])], axis=1)
    layer_out = whole(out_near, out_far)
    grad_tokens = whole(grad_near, grad_far)
    totals = gather(gather(totals, "ylo"), "z").reshape(nodes * few, 2 * width)
    sum_out = totals[:, :width].astype(jnp.float32)
    sum_in = totals[:, width:].reshape(nodes, few, slab // few, half).swapaxes(1, 2)
    sum_in = sum_in.reshape(2, -1, half)
    in_keep = lax.dynamic_index_in_dim(sum_in, core, 0, keepdims=False)
    in_got = swap(lax.dynamic_index_in_dim(sum_in, 1 - core, 0, keepdims=False))
    sum_in = contract_cols(jnp.concatenate([in_keep, in_got], axis=1), picking)
    return (layer_out, grad_tokens, grad_upper[None], grad_lower[None], sum_in, sum_out)


def solution(mesh):
    node, local = mesh.shape["node"], mesh.shape["local"]
    fine = Mesh(mesh.devices.reshape(node // 2, 2, local // 4, 2, 2), AXES)
    every = AXES
    shared = ("x", "yhi", "core")
    return jax.shard_map(
        body,
        mesh=fine,
        in_specs=(
            P(every, None),
            P(every, None),
            P(every),
            P(every, None),
            P(every, None, None),
            P(every, None, None),
            P(shared, None),
            P(shared, None),
        ),
        out_specs=(
            P(every, None),
            P(every, None),
            P(every, None, None),
            P(every, None, None),
            P(shared, None),
            P(shared, None),
        ),
        check_vma=False,
    )
```

```python
import jax
import jax.numpy as jnp
from jax import lax
from jax.sharding import Mesh, PartitionSpec as P

half_root = 0.7071067811865476
inv_root_tau = 0.3989422804014327

AXES = ("z", "ylo", "x", "yhi", "core")
CHIPS = ("z", "ylo", "x", "yhi")


def gelu_value(values):
    return 0.5 * values * (1.0 + lax.erf(values * half_root))


def gelu_slope(values):
    return 0.5 * (1.0 + lax.erf(values * half_root)) + values * inv_root_tau * jnp.exp(
        -0.5 * values * values
    )


def dot(left, right):
    return jnp.dot(left, right, preferred_element_type=jnp.float32)


def contract_rows(left, right):
    return lax.dot_general(
        left, right, (((0,), (0,)), ((), ())), preferred_element_type=jnp.float32
    )


def contract_cols(left, right):
    return lax.dot_general(
        left, right, (((1,), (1,)), ((), ())), preferred_element_type=jnp.float32
    )


def together(*arrays):
    return lax.optimization_barrier(arrays)


def swap(values):
    return lax.ppermute(values, "core", [(0, 1), (1, 0)])


def gather(values, axis):
    count = lax.axis_size(axis)
    here = lax.axis_index(axis)
    out = jnp.zeros((count,) + values.shape, values.dtype)
    zeros = (0,) * values.ndim
    for step in range(count):
        piece = values
        if step:
            piece = lax.ppermute(values, axis, [((i + step) % count, i) for i in range(count)])
        out = lax.dynamic_update_slice(out, piece[None], (lax.rem(here + step, count),) + zeros)
    return out


def exchange(values):
    return lax.all_to_all(values, CHIPS, split_axis=0, concat_axis=0, tiled=True)


def body(tokens, expert_ids, gate_code, grad_out, up_weight, down_weight, shared_up, shared_down):
    core = lax.axis_index("core")
    rows, width = tokens.shape
    chips = lax.axis_size("z") * lax.axis_size("ylo") * lax.axis_size("x") * lax.axis_size("yhi")
    cap = 4 * rows // (2 * chips)
    slots = chips * 2 * cap

    chip_tokens = jnp.concatenate([tokens, swap(tokens)], axis=0)
    chip_grads = jnp.concatenate([grad_out, swap(grad_out)], axis=0)

    id_rows = expert_ids.T
    order = jnp.arange(rows, dtype=jnp.int32)
    earlier = order[:, None] < order[None, :]
    positions = []
    for column in range(2):
        same = (expert_ids[:, 0:1] == id_rows[column : column + 1]) | (
            expert_ids[:, 1:2] == id_rows[column : column + 1]
        )
        positions.append(jnp.sum((same & earlier).astype(jnp.int32), axis=0))
    routes = jnp.stack(
        [id_rows[0] * cap + positions[0], id_rows[1] * cap + positions[1], gate_code]
    )
    routes_other = swap(routes)

    def targets(packed, offset):
        expert = packed[:2] // cap
        position = packed[:2] - expert * cap
        slot = (expert // 2) * (2 * cap) + offset + position
        return jnp.where(expert - (expert // 2) * 2 == core, slot, -1)

    target = jnp.concatenate([targets(routes, 0), targets(routes_other, cap)], axis=1)
    first_gate = jnp.concatenate([routes[2], routes_other[2]]).astype(jnp.float32) / 8.0
    slot_grid = jnp.arange(slots, dtype=jnp.int32)[:, None]
    hit_first = slot_grid == target[0][None, :]
    hit_second = slot_grid == target[1][None, :]
    placing = (hit_first | hit_second).astype(jnp.bfloat16)
    weighing = (
        jnp.where(hit_first, first_gate[None, :], 0.0)
        + jnp.where(hit_second, 1.0 - first_gate[None, :], 0.0)
    ).astype(jnp.bfloat16)


    hidden_rows = shared_down.shape[0]
    groups = shared_up.shape[1] // (2 * hidden_rows)
    nodes = lax.axis_size("z") * lax.axis_size("ylo")
    few = hidden_rows // nodes
    half = groups * hidden_rows
    unit = jnp.arange(2 * half, dtype=jnp.int32)
    inner = lax.rem(unit, half)
    side = jnp.where(unit < half, core, 1 - core)
    picked = (lax.rem(inner // few, groups) * 2 + side) * hidden_rows
    picked = picked + (inner // (groups * few)) * few + lax.rem(inner, few)
    picking = (unit[:, None] == picked[None, :]).astype(jnp.bfloat16)
    by_core = dot(shared_up, picking).astype(jnp.bfloat16)
    up_keep, up_got = by_core[:, :half], swap(by_core[:, half:])
    up_chip = jnp.where(
        core == 0,
        jnp.concatenate([up_keep, up_got], axis=0),
        jnp.concatenate([up_got, up_keep], axis=0),
    )
    node = lax.axis_index("z") * lax.axis_size("ylo") + lax.axis_index("ylo")
    slab = width // (groups * nodes)
    up_slab = lax.dynamic_slice_in_dim(up_chip, node * slab, slab, 0)
    up_slab = up_slab.reshape(slab // few, few, half).swapaxes(0, 1).reshape(few, width)
    down_slab = lax.dynamic_slice_in_dim(shared_down, node * few, few, 0)

    def copies(slab_rows):
        return jnp.broadcast_to(slab_rows[None], (chips, few, width)).reshape(chips * few, width)

    payload = jnp.concatenate(
        [dot(placing, chip_tokens).astype(jnp.bfloat16), copies(up_slab), copies(down_slab)], axis=1
    )
    payload, chip_grads = together(payload, chip_grads)
    arrived_both = exchange(payload)
    upstream = exchange(dot(weighing, chip_grads).astype(jnp.bfloat16))
    arrived = arrived_both[:, :width]
    shared_back_out = arrived_both[:, 2 * width :]
    shared_in = arrived_both[:, width : 2 * width].reshape(nodes, groups, few, slab // few, half)
    shared_in = shared_in.transpose(1, 0, 3, 2, 4).reshape(width, half)

    shared_pre = dot(chip_tokens, shared_in)
    shared_hidden = gelu_value(shared_pre).astype(jnp.bfloat16)
    shared_back = contract_cols(chip_grads, shared_back_out)
    shared_slopes = (shared_back * gelu_slope(shared_pre)).astype(jnp.bfloat16)
    term_out = contract_rows(shared_hidden, chip_grads).astype(jnp.bfloat16)
    term_in = contract_rows(chip_tokens, shared_slopes).astype(jnp.bfloat16)
    term_in = term_in.reshape(groups, nodes, slab // few, few, half).transpose(1, 0, 3, 2, 4)

    upward = up_weight[0]
    downward = down_weight[0]
    preact = dot(arrived, upward)
    hidden = gelu_value(preact).astype(jnp.bfloat16)
    produced = dot(hidden, downward).astype(jnp.bfloat16)
    back = jnp.concatenate([produced, term_out, term_in.reshape(half, width)], axis=1)
    back, upstream = together(back, upstream)
    returned = exchange(back)
    hidden_grad = contract_cols(upstream, downward)
    slopes = (hidden_grad * gelu_slope(preact)).astype(jnp.bfloat16)
    inward = contract_cols(slopes, upward).astype(jnp.bfloat16)

    def parts_of(routing, rows_back, shared_part):
        near = contract_rows(routing[:, :rows], rows_back) + shared_part[:rows]
        far = contract_rows(routing[:, rows:], rows_back) + shared_part[rows:]
        return near, far.astype(jnp.bfloat16)

    def whole(near, far):
        return (near + swap(far).astype(jnp.float32)).astype(jnp.bfloat16)

    totals = returned[:, width:].reshape(chips, few, 2 * width).astype(jnp.float32)
    totals = gather(totals.sum(axis=0).astype(jnp.bfloat16), "ylo")
    inward, totals = together(inward, totals)
    landed = exchange(inward)
    totals = gather(totals, "z").reshape(nodes * few, 2 * width)
    totals, returned, slopes = together(totals, returned, slopes)

    out_near, out_far = parts_of(weighing, returned[:, :width], dot(shared_hidden, shared_back_out))
    shared_grad = contract_cols(shared_slopes, shared_in)
    out_near, out_far, shared_grad, slopes = together(out_near, out_far, shared_grad, slopes)
    grad_upper = contract_rows(arrived, slopes).astype(jnp.bfloat16)
    grad_lower = contract_rows(hidden, upstream).astype(jnp.bfloat16)
    landed, grad_upper, grad_lower = together(landed, grad_upper, grad_lower)
    grad_near, grad_far = parts_of(placing, landed, shared_grad)
    layer_out = whole(out_near, out_far)
    grad_tokens = whole(grad_near, grad_far)
    sum_out = totals[:, :width].astype(jnp.float32)
    sum_in = totals[:, width:].reshape(nodes, few, slab // few, half).swapaxes(1, 2)
    sum_in = sum_in.reshape(2, -1, half)
    in_keep = lax.dynamic_index_in_dim(sum_in, core, 0, keepdims=False)
    in_got = swap(lax.dynamic_index_in_dim(sum_in, 1 - core, 0, keepdims=False))
    sum_in = contract_cols(jnp.concatenate([in_keep, in_got], axis=1), picking)
    return (layer_out, grad_tokens, grad_upper[None], grad_lower[None], sum_in, sum_out)


def solution(mesh):
    node, local = mesh.shape["node"], mesh.shape["local"]
    fine = Mesh(mesh.devices.reshape(node // 2, 2, local // 4, 2, 2), AXES)
    every = AXES
    shared = ("x", "yhi", "core")
    return jax.shard_map(
        body,
        mesh=fine,
        in_specs=(
            P(every, None),
            P(every, None),
            P(every),
            P(every, None),
            P(every, None, None),
            P(every, None, None),
            P(shared, None),
            P(shared, None),
        ),
        out_specs=(
            P(every, None),
            P(every, None),
            P(every, None, None),
            P(every, None, None),
            P(shared, None),
            P(shared, None),
        ),
        check_vma=False,
    )
```

```python
import math

import numpy as np
import jax
import jax.numpy as jnp
from jax import lax
from jax.sharding import Mesh, PartitionSpec as P

half_root = 0.7071067811865476
inv_root_tau = 0.3989422804014327

AXES = ("z", "ylo", "x", "yhi", "core")
CHIPS = ("z", "ylo", "x", "yhi")


def gelu_value(values):
    return 0.5 * values * (1.0 + lax.erf(values * half_root))


def gelu_slope(values):
    return 0.5 * (1.0 + lax.erf(values * half_root)) + values * inv_root_tau * jnp.exp(
        -0.5 * values * values
    )


def dot(left, right):
    return jnp.dot(left, right, preferred_element_type=jnp.float32)


def contract_rows(left, right):
    return lax.dot_general(
        left, right, (((0,), (0,)), ((), ())), preferred_element_type=jnp.float32
    )


def contract_cols(left, right):
    return lax.dot_general(
        left, right, (((1,), (1,)), ((), ())), preferred_element_type=jnp.float32
    )


def together(*arrays):
    return lax.optimization_barrier(arrays)


def swap(values):
    return lax.ppermute(values, "core", [(0, 1), (1, 0)])


def place_of(axes):
    place = 0
    for axis in axes:
        place = place * lax.axis_size(axis) + lax.axis_index(axis)
    return place


def count_of(axes):
    count = 1
    for axis in axes:
        count *= lax.axis_size(axis)
    return count


def collect(values, axis):
    count = lax.axis_size(axis)
    return jnp.stack(
        [values]
        + [
            lax.ppermute(values, axis, [((i + step) % count, i) for i in range(count)])
            for step in range(1, count)
        ]
    )


def in_order(blocks, axes):
    sizes = [lax.axis_size(axis) for axis in axes]
    heres = [lax.axis_index(axis) for axis in axes]
    out = jnp.zeros_like(blocks)
    rest = blocks.ndim - len(axes)
    for index in range(math.prod(sizes)):
        steps = np.unravel_index(index, sizes)
        at = [lax.rem(here + int(k), size) for here, k, size in zip(heres, steps, sizes)]
        block = blocks[tuple(slice(int(k), int(k) + 1) for k in steps)]
        out = lax.dynamic_update_slice(out, block, tuple(at) + (0,) * rest)
    return out


def scatter_sum(own, others, axis):
    count = lax.axis_size(axis)
    total = own.astype(jnp.float32)
    for step in range(1, count):
        got = lax.ppermute(
            others[step - 1].astype(jnp.bfloat16), axis, [(i, (i + step) % count) for i in range(count)]
        )
        total = total + got.astype(jnp.float32)
    return total


def by_distance(values, axis):
    count = lax.axis_size(axis)
    here = lax.axis_index(axis)
    return [
        lax.dynamic_index_in_dim(values, lax.rem(here + step, count), 0, keepdims=False)
        for step in range(count)
    ]


def exchange(values):
    return lax.all_to_all(values, CHIPS, split_axis=0, concat_axis=0, tiled=True)


def body(tokens, expert_ids, gate_code, grad_out, up_weight, down_weight, shared_up, shared_down):
    core = lax.axis_index("core")
    rows, width = tokens.shape
    chips = lax.axis_size("z") * lax.axis_size("ylo") * lax.axis_size("x") * lax.axis_size("yhi")
    cap = 4 * rows // (2 * chips)
    slots = chips * 2 * cap

    hidden_rows = shared_down.shape[0]
    groups = shared_up.shape[1] // (2 * hidden_rows)
    half = groups * hidden_rows
    unit = jnp.arange(2 * half, dtype=jnp.int32)
    inner = lax.rem(unit, half)
    side = jnp.where(unit < half, core, 1 - core)
    picked = (inner // hidden_rows * 2 + side) * hidden_rows + lax.rem(inner, hidden_rows)
    picking = (unit[:, None] == picked[None, :]).astype(jnp.bfloat16)
    by_core = dot(shared_up, picking).astype(jnp.bfloat16)
    up_keep, up_got = by_core[:, :half], swap(by_core[:, half:])

    quarters, x_count, yhi_count = lax.axis_size("z"), lax.axis_size("x"), lax.axis_size("yhi")
    few = hidden_rows // quarters
    piece = lax.dynamic_slice_in_dim(shared_down, lax.axis_index("z") * few, few, 0)
    piece = collect(piece, "yhi")
    expert_ids, up_got, piece, tokens_other, grads_other = together(
        expert_ids, up_got, piece, swap(tokens), swap(grad_out)
    )
    up_chip = jnp.where(
        core == 0,
        jnp.concatenate([up_keep, up_got], axis=0),
        jnp.concatenate([up_got, up_keep], axis=0),
    )
    up_pair = collect(up_chip, "yhi")
    piece = collect(piece, "x")

    chip_tokens = jnp.concatenate([tokens, tokens_other], axis=0)
    chip_grads = jnp.concatenate([grad_out, grads_other], axis=0)

    id_rows = expert_ids.T
    order = jnp.arange(rows, dtype=jnp.int32)
    earlier = order[:, None] < order[None, :]
    positions = []
    for column in range(2):
        same = (expert_ids[:, 0:1] == id_rows[column : column + 1]) | (
            expert_ids[:, 1:2] == id_rows[column : column + 1]
        )
        positions.append(jnp.sum((same & earlier).astype(jnp.int32), axis=0))
    routes = jnp.stack(
        [id_rows[0] * cap + positions[0], id_rows[1] * cap + positions[1], gate_code]
    )
    routes_other = swap(routes)

    def targets(packed, offset):
        expert = packed[:2] // cap
        position = packed[:2] - expert * cap
        slot = (expert // 2) * (2 * cap) + offset + position
        return jnp.where(expert - (expert // 2) * 2 == core, slot, -1)

    target = jnp.concatenate([targets(routes, 0), targets(routes_other, cap)], axis=1)
    first_gate = jnp.concatenate([routes[2], routes_other[2]]).astype(jnp.float32) / 8.0
    slot_grid = jnp.arange(slots, dtype=jnp.int32)[:, None]
    hit_first = slot_grid == target[0][None, :]
    hit_second = slot_grid == target[1][None, :]
    placing = (hit_first | hit_second).astype(jnp.bfloat16)
    weighing = (
        jnp.where(hit_first, first_gate[None, :], 0.0)
        + jnp.where(hit_second, 1.0 - first_gate[None, :], 0.0)
    ).astype(jnp.bfloat16)

    payload = dot(placing, chip_tokens).astype(jnp.bfloat16)
    payload, chip_grads, up_pair, piece = together(payload, chip_grads, up_pair, piece)
    arrived = exchange(payload)
    upstream = exchange(dot(weighing, chip_grads).astype(jnp.bfloat16))
    shared_in = in_order(collect(up_pair, "x"), ("x", "yhi")).reshape(width, half)
    shared_back_out = collect(piece, "z").reshape(half, width)

    arrived, shared_in, shared_back_out = together(arrived, shared_in, shared_back_out)

    place = jnp.arange(half, dtype=jnp.int32)
    sizes = (quarters, x_count, yhi_count, few)
    steps = []
    for size in reversed(sizes):
        steps.append(lax.rem(place, size))
        place = place // size
    row, on_yhi, on_x, on_z = steps
    on_yhi = lax.rem(on_yhi + lax.axis_index("yhi"), yhi_count)
    on_x = lax.rem(on_x + lax.axis_index("x"), x_count)
    on_z = lax.rem(on_z + lax.axis_index("z"), quarters)
    natural = ((on_x * yhi_count + on_yhi) * quarters + on_z) * few + row
    turning = (jnp.arange(half, dtype=jnp.int32)[:, None] == natural[None, :]).astype(jnp.bfloat16)
    turned_in = dot(shared_in, turning).astype(jnp.bfloat16)

    shared_pre = dot(chip_tokens, turned_in)
    shared_hidden = gelu_value(shared_pre).astype(jnp.bfloat16)
    shared_back = contract_cols(chip_grads, shared_back_out)
    shared_slopes = (shared_back * gelu_slope(shared_pre)).astype(jnp.bfloat16)
    term_out = contract_rows(shared_hidden, chip_grads).astype(jnp.bfloat16)
    natural_slopes = contract_cols(shared_slopes, turning).astype(jnp.bfloat16)
    term_in = contract_rows(chip_tokens, natural_slopes).astype(jnp.bfloat16)

    near_in, *far_in = by_distance(term_in.reshape(x_count, -1, half), "x")
    part_in = scatter_sum(near_in, far_in, "x")
    term_out = term_out.reshape(quarters, -1, width)
    part_out = scatter_sum(term_out[0], term_out[1:], "z")

    upward = up_weight[0]
    downward = down_weight[0]
    preact = dot(arrived, upward)
    hidden = gelu_value(preact).astype(jnp.bfloat16)
    produced = dot(hidden, downward).astype(jnp.bfloat16)
    returned = exchange(produced)
    upstream, part_in, part_out = together(upstream, part_in, part_out)
    hidden_grad = contract_cols(upstream, downward)
    slopes = (hidden_grad * gelu_slope(preact)).astype(jnp.bfloat16)
    inward = contract_cols(slopes, upward).astype(jnp.bfloat16)

    part_in = part_in.reshape(yhi_count, 2, quarters, -1, half).transpose(2, 0, 1, 3, 4)
    near_in, *far_in = by_distance(part_in, "z")
    part_in = scatter_sum(near_in, far_in, "z").reshape(yhi_count, -1, half)
    part_out = part_out.reshape(x_count, yhi_count, -1, width)
    part_out = scatter_sum(part_out[0], part_out[1:], "x")
    part_in = jnp.stack(by_distance(part_in, "yhi"))
    part = jnp.stack([part_in, part_out.reshape(part_in.shape)], axis=1).astype(jnp.bfloat16)

    part, inward = together(part, inward)

    along_y = ("ylo", "yhi")
    ring = count_of(along_y)
    here = place_of(along_y)
    parts = jnp.zeros((ring,) + part.shape[1:], part.dtype)
    for step in range(ring):
        target = lax.rem(here + step, ring)
        got = lax.dynamic_index_in_dim(
            part, lax.rem(target + here, yhi_count), 0, keepdims=False
        )
        if step:
            got = lax.ppermute(got, along_y, [(i, (i + step) % ring) for i in range(ring)])
        origin = lax.rem(here + ring - step, ring)
        parts = lax.dynamic_update_slice(parts, got[None], (origin, 0, 0, 0))
    parts = parts.astype(jnp.float32).sum(axis=0).astype(jnp.bfloat16)
    inward, parts, upstream = together(inward, parts, upstream)
    landed = exchange(inward)

    parts = in_order(collect(parts, "z"), ("z",))
    parts, returned = together(parts, returned)
    sum_out = parts[:, 1].reshape(shared_down.shape).astype(jnp.float32)
    both = parts[:, 0].reshape(quarters, 2, -1, half).swapaxes(0, 1).reshape(2, -1, half)
    in_keep = lax.dynamic_index_in_dim(both, core, 0, keepdims=False)
    in_got = swap(lax.dynamic_index_in_dim(both, 1 - core, 0, keepdims=False))
    sum_in = contract_cols(jnp.concatenate([in_keep, in_got], axis=1), picking)

    def parts_of(routing, rows_back, shared_part):
        near = contract_rows(routing[:, :rows], rows_back) + shared_part[:rows]
        far = contract_rows(routing[:, rows:], rows_back) + shared_part[rows:]
        return near, far.astype(jnp.bfloat16)

    def whole(near, far):
        return (near + swap(far).astype(jnp.float32)).astype(jnp.bfloat16)

    out_near, out_far = parts_of(weighing, returned, dot(shared_hidden, shared_back_out))
    shared_grad = contract_cols(shared_slopes, turned_in)
    out_near, out_far, shared_grad, slopes = together(out_near, out_far, shared_grad, slopes)
    grad_upper = contract_rows(arrived, slopes).astype(jnp.bfloat16)
    grad_lower = contract_rows(hidden, upstream).astype(jnp.bfloat16)
    landed, grad_upper, grad_lower = together(landed, grad_upper, grad_lower)
    grad_near, grad_far = parts_of(placing, landed, shared_grad)
    layer_out = whole(out_near, out_far)
    grad_tokens = whole(grad_near, grad_far)
    return (layer_out, grad_tokens, grad_upper[None], grad_lower[None], sum_in, sum_out)


def solution(mesh):
    node, local = mesh.shape["node"], mesh.shape["local"]
    fine = Mesh(mesh.devices.reshape(node // 2, 2, local // 4, 2, 2), AXES)
    every = AXES
    shared = ("x", "yhi", "core")
    return jax.shard_map(
        body,
        mesh=fine,
        in_specs=(
            P(every, None),
            P(every, None),
            P(every),
            P(every, None),
            P(every, None, None),
            P(every, None, None),
            P(shared, None),
            P(shared, None),
        ),
        out_specs=(
            P(every, None),
            P(every, None),
            P(every, None, None),
            P(every, None, None),
            P(shared, None),
            P(shared, None),
        ),
        check_vma=False,
    )
```

```python
import math

import numpy as np
import jax
import jax.numpy as jnp
from jax import lax
from jax.sharding import Mesh, PartitionSpec as P

half_root = 0.7071067811865476
inv_root_tau = 0.3989422804014327

AXES = ("z", "ylo", "x", "yhi", "core")
CHIPS = ("z", "ylo", "x", "yhi")


def gelu_value(values):
    return 0.5 * values * (1.0 + lax.erf(values * half_root))


def gelu_slope(values):
    return 0.5 * (1.0 + lax.erf(values * half_root)) + values * inv_root_tau * jnp.exp(
        -0.5 * values * values
    )


def dot(left, right):
    return jnp.dot(left, right, preferred_element_type=jnp.float32)


def contract_rows(left, right):
    return lax.dot_general(
        left, right, (((0,), (0,)), ((), ())), preferred_element_type=jnp.float32
    )


def contract_cols(left, right):
    return lax.dot_general(
        left, right, (((1,), (1,)), ((), ())), preferred_element_type=jnp.float32
    )


def together(*arrays):
    return lax.optimization_barrier(arrays)


def swap(values):
    return lax.ppermute(values, "core", [(0, 1), (1, 0)])


def place_of(axes):
    place = 0
    for axis in axes:
        place = place * lax.axis_size(axis) + lax.axis_index(axis)
    return place


def count_of(axes):
    count = 1
    for axis in axes:
        count *= lax.axis_size(axis)
    return count


def collect(values, axis):
    count = lax.axis_size(axis)
    return jnp.stack(
        [values]
        + [
            lax.ppermute(values, axis, [((i + step) % count, i) for i in range(count)])
            for step in range(1, count)
        ]
    )


def in_order(blocks, axes):
    sizes = [lax.axis_size(axis) for axis in axes]
    heres = [lax.axis_index(axis) for axis in axes]
    out = jnp.zeros_like(blocks)
    rest = blocks.ndim - len(axes)
    for index in range(math.prod(sizes)):
        steps = np.unravel_index(index, sizes)
        at = [lax.rem(here + int(k), size) for here, k, size in zip(heres, steps, sizes)]
        block = blocks[tuple(slice(int(k), int(k) + 1) for k in steps)]
        out = lax.dynamic_update_slice(out, block, tuple(at) + (0,) * rest)
    return out


def scatter_sum(own, others, axis):
    count = lax.axis_size(axis)
    total = own.astype(jnp.float32)
    for step in range(1, count):
        got = lax.ppermute(
            others[step - 1].astype(jnp.bfloat16), axis, [(i, (i + step) % count) for i in range(count)]
        )
        total = total + got.astype(jnp.float32)
    return total


def by_distance(values, axis):
    count = lax.axis_size(axis)
    here = lax.axis_index(axis)
    return [
        lax.dynamic_index_in_dim(values, lax.rem(here + step, count), 0, keepdims=False)
        for step in range(count)
    ]


def exchange(values):
    return lax.all_to_all(values, CHIPS, split_axis=0, concat_axis=0, tiled=True)


def body(tokens, expert_ids, gate_code, grad_out, up_weight, down_weight, shared_up, shared_down):
    core = lax.axis_index("core")
    rows, width = tokens.shape
    chips = lax.axis_size("z") * lax.axis_size("ylo") * lax.axis_size("x") * lax.axis_size("yhi")
    cap = 4 * rows // (2 * chips)
    slots = chips * 2 * cap

    hidden_rows = shared_down.shape[0]
    groups = shared_up.shape[1] // (2 * hidden_rows)
    half = groups * hidden_rows
    unit = jnp.arange(2 * half, dtype=jnp.int32)
    inner = lax.rem(unit, half)
    side = jnp.where(unit < half, core, 1 - core)
    picked = (inner // hidden_rows * 2 + side) * hidden_rows + lax.rem(inner, hidden_rows)
    picking = (unit[:, None] == picked[None, :]).astype(jnp.bfloat16)
    by_core = dot(shared_up, picking).astype(jnp.bfloat16)
    up_keep, up_send = by_core[:, :half], by_core[:, half:]
    up_near = swap(up_send)
    up_far = lax.ppermute(up_keep, "yhi", [(0, 1), (1, 0)])
    up_cross = lax.ppermute(up_send, ("yhi", "core"), [(i, 3 - i) for i in range(4)])

    quarters, x_count, yhi_count = lax.axis_size("z"), lax.axis_size("x"), lax.axis_size("yhi")
    few = hidden_rows // quarters
    piece = lax.dynamic_slice_in_dim(shared_down, lax.axis_index("z") * few, few, 0)
    piece = collect(piece, "yhi")
    expert_ids, piece, tokens_other, grads_other, up_near, up_far, up_cross = together(
        expert_ids, piece, swap(tokens), swap(grad_out), up_near, up_far, up_cross
    )
    piece = collect(piece, "x")

    def by_rows(same, other):
        return jnp.where(
            core == 0,
            jnp.concatenate([same, other], axis=0),
            jnp.concatenate([other, same], axis=0),
        )

    up_pair = jnp.stack([by_rows(up_keep, up_near), by_rows(up_far, up_cross)])
    up_full = collect(up_pair, "x")

    chip_tokens = jnp.concatenate([tokens, tokens_other], axis=0)
    chip_grads = jnp.concatenate([grad_out, grads_other], axis=0)

    id_rows = expert_ids.T
    order = jnp.arange(rows, dtype=jnp.int32)
    earlier = order[:, None] < order[None, :]
    positions = []
    for column in range(2):
        same = (expert_ids[:, 0:1] == id_rows[column : column + 1]) | (
            expert_ids[:, 1:2] == id_rows[column : column + 1]
        )
        positions.append(jnp.sum((same & earlier).astype(jnp.int32), axis=0))
    routes = jnp.stack(
        [id_rows[0] * cap + positions[0], id_rows[1] * cap + positions[1], gate_code]
    )
    routes_other = swap(routes)

    def targets(packed, offset):
        expert = packed[:2] // cap
        position = packed[:2] - expert * cap
        slot = (expert // 2) * (2 * cap) + offset + position
        return jnp.where(expert - (expert // 2) * 2 == core, slot, -1)

    target = jnp.concatenate([targets(routes, 0), targets(routes_other, cap)], axis=1)
    first_gate = jnp.concatenate([routes[2], routes_other[2]]).astype(jnp.float32) / 8.0
    slot_grid = jnp.arange(slots, dtype=jnp.int32)[:, None]
    hit_first = slot_grid == target[0][None, :]
    hit_second = slot_grid == target[1][None, :]
    placing = (hit_first | hit_second).astype(jnp.bfloat16)
    weighing = (
        jnp.where(hit_first, first_gate[None, :], 0.0)
        + jnp.where(hit_second, 1.0 - first_gate[None, :], 0.0)
    ).astype(jnp.bfloat16)

    payload = dot(placing, chip_tokens).astype(jnp.bfloat16)
    payload, chip_grads, piece = together(payload, chip_grads, piece)
    arrived = exchange(payload)
    upstream = exchange(dot(weighing, chip_grads).astype(jnp.bfloat16))
    shared_in = in_order(up_full, ("x", "yhi")).reshape(width, half)
    shared_back_out = collect(piece, "z").reshape(half, width)

    arrived, shared_in, shared_back_out = together(arrived, shared_in, shared_back_out)

    place = jnp.arange(half, dtype=jnp.int32)
    sizes = (quarters, x_count, yhi_count, few)
    steps = []
    for size in reversed(sizes):
        steps.append(lax.rem(place, size))
        place = place // size
    row, on_yhi, on_x, on_z = steps
    on_yhi = lax.rem(on_yhi + lax.axis_index("yhi"), yhi_count)
    on_x = lax.rem(on_x + lax.axis_index("x"), x_count)
    on_z = lax.rem(on_z + lax.axis_index("z"), quarters)
    natural = ((on_x * yhi_count + on_yhi) * quarters + on_z) * few + row
    turning = (jnp.arange(half, dtype=jnp.int32)[:, None] == natural[None, :]).astype(jnp.bfloat16)
    turned_in = dot(shared_in, turning).astype(jnp.bfloat16)

    shared_pre = dot(chip_tokens, turned_in)
    shared_hidden = gelu_value(shared_pre).astype(jnp.bfloat16)
    shared_back = contract_cols(chip_grads, shared_back_out)
    shared_slopes = (shared_back * gelu_slope(shared_pre)).astype(jnp.bfloat16)
    term_out = contract_rows(shared_hidden, chip_grads).astype(jnp.bfloat16)
    natural_slopes = contract_cols(shared_slopes, turning).astype(jnp.bfloat16)
    term_in = contract_rows(chip_tokens, natural_slopes).astype(jnp.bfloat16)

    near_in, *far_in = by_distance(term_in.reshape(x_count, -1, half), "x")
    part_in = scatter_sum(near_in, far_in, "x")
    term_out = term_out.reshape(quarters, -1, width)
    part_out = scatter_sum(term_out[0], term_out[1:], "z")

    upward = up_weight[0]
    downward = down_weight[0]
    preact = dot(arrived, upward)
    hidden = gelu_value(preact).astype(jnp.bfloat16)
    produced = dot(hidden, downward).astype(jnp.bfloat16)
    returned = exchange(produced)
    upstream, part_in, part_out = together(upstream, part_in, part_out)
    hidden_grad = contract_cols(upstream, downward)
    slopes = (hidden_grad * gelu_slope(preact)).astype(jnp.bfloat16)
    inward = contract_cols(slopes, upward).astype(jnp.bfloat16)

    part_in = part_in.reshape(yhi_count, 2, quarters, -1, half).transpose(2, 0, 1, 3, 4)
    near_in, *far_in = by_distance(part_in, "z")
    part_in = scatter_sum(near_in, far_in, "z").reshape(yhi_count, -1, half)
    part_out = part_out.reshape(x_count, yhi_count, -1, width)
    part_out = scatter_sum(part_out[0], part_out[1:], "x")
    part_in = jnp.stack(by_distance(part_in, "yhi"))
    part = jnp.stack([part_in, part_out.reshape(part_in.shape)], axis=1).astype(jnp.bfloat16)

    part, inward = together(part, inward)

    along_y = ("ylo", "yhi")
    ring = count_of(along_y)
    here = place_of(along_y)
    parts = jnp.zeros((ring,) + part.shape[1:], part.dtype)
    for step in range(ring):
        target = lax.rem(here + step, ring)
        got = lax.dynamic_index_in_dim(
            part, lax.rem(target + here, yhi_count), 0, keepdims=False
        )
        if step:
            got = lax.ppermute(got, along_y, [(i, (i + step) % ring) for i in range(ring)])
        origin = lax.rem(here + ring - step, ring)
        parts = lax.dynamic_update_slice(parts, got[None], (origin, 0, 0, 0))
    parts = parts.astype(jnp.float32).sum(axis=0).astype(jnp.bfloat16)
    inward, parts, returned = together(inward, parts, returned)
    landed = exchange(inward)

    parts = in_order(collect(parts, "z"), ("z",))
    parts, returned, upstream, shared_hidden, shared_slopes = together(
        parts, returned, upstream, shared_hidden, shared_slopes
    )
    sum_out = parts[:, 1].reshape(shared_down.shape).astype(jnp.float32)
    both = parts[:, 0].reshape(quarters, 2, -1, half).swapaxes(0, 1).reshape(2, -1, half)
    in_keep = lax.dynamic_index_in_dim(both, core, 0, keepdims=False)
    in_got = swap(lax.dynamic_index_in_dim(both, 1 - core, 0, keepdims=False))
    sum_in = contract_cols(jnp.concatenate([in_keep, in_got], axis=1), picking)

    def parts_of(routing, rows_back, shared_part):
        near = contract_rows(routing[:, :rows], rows_back) + shared_part[:rows]
        far = contract_rows(routing[:, rows:], rows_back) + shared_part[rows:]
        return near, far.astype(jnp.bfloat16)

    def whole(near, far):
        return (near + swap(far).astype(jnp.float32)).astype(jnp.bfloat16)

    out_near, out_far = parts_of(weighing, returned, dot(shared_hidden, shared_back_out))
    shared_grad = contract_cols(shared_slopes, turned_in)
    out_near, out_far, shared_grad, slopes = together(out_near, out_far, shared_grad, slopes)
    grad_upper = contract_rows(arrived, slopes).astype(jnp.bfloat16)
    grad_lower = contract_rows(hidden, upstream).astype(jnp.bfloat16)
    landed, grad_upper, grad_lower = together(landed, grad_upper, grad_lower)
    grad_near, grad_far = parts_of(placing, landed, shared_grad)
    layer_out = whole(out_near, out_far)
    grad_tokens = whole(grad_near, grad_far)
    return (layer_out, grad_tokens, grad_upper[None], grad_lower[None], sum_in, sum_out)


def solution(mesh):
    node, local = mesh.shape["node"], mesh.shape["local"]
    fine = Mesh(mesh.devices.reshape(node // 2, 2, local // 4, 2, 2), AXES)
    every = AXES
    shared = ("x", "yhi", "core")
    return jax.shard_map(
        body,
        mesh=fine,
        in_specs=(
            P(every, None),
            P(every, None),
            P(every),
            P(every, None),
            P(every, None, None),
            P(every, None, None),
            P(shared, None),
            P(shared, None),
        ),
        out_specs=(
            P(every, None),
            P(every, None),
            P(every, None, None),
            P(every, None, None),
            P(shared, None),
            P(shared, None),
        ),
        check_vma=False,
    )
```

```python
import math

import numpy as np
import jax
import jax.numpy as jnp
from jax import lax
from jax.sharding import Mesh, PartitionSpec as P

half_root = 0.7071067811865476
inv_root_tau = 0.3989422804014327

AXES = ("z", "ylo", "x", "yhi", "core")
CHIPS = ("z", "ylo", "x", "yhi")


def gelu_value(values):
    return 0.5 * values * (1.0 + lax.erf(values * half_root))


def gelu_slope(values):
    return 0.5 * (1.0 + lax.erf(values * half_root)) + values * inv_root_tau * jnp.exp(
        -0.5 * values * values
    )


def dot(left, right):
    return jnp.dot(left, right, preferred_element_type=jnp.float32)


def contract_rows(left, right):
    return lax.dot_general(
        left, right, (((0,), (0,)), ((), ())), preferred_element_type=jnp.float32
    )


def contract_cols(left, right):
    return lax.dot_general(
        left, right, (((1,), (1,)), ((), ())), preferred_element_type=jnp.float32
    )


def together(*arrays):
    return lax.optimization_barrier(arrays)


def swap(values):
    return lax.ppermute(values, "core", [(0, 1), (1, 0)])


def place_of(axes):
    place = 0
    for axis in axes:
        place = place * lax.axis_size(axis) + lax.axis_index(axis)
    return place


def count_of(axes):
    count = 1
    for axis in axes:
        count *= lax.axis_size(axis)
    return count


def pieces(values, axis):
    count = lax.axis_size(axis)
    return [values] + [
        lax.ppermute(values, axis, [((i + step) % count, i) for i in range(count)])
        for step in range(1, count)
    ]


def collect(values, axis):
    return jnp.stack(pieces(values, axis))


def in_order(blocks, axes):
    sizes = [lax.axis_size(axis) for axis in axes]
    heres = [lax.axis_index(axis) for axis in axes]
    out = jnp.zeros_like(blocks)
    rest = blocks.ndim - len(axes)
    for index in range(math.prod(sizes)):
        steps = np.unravel_index(index, sizes)
        at = [lax.rem(here + int(k), size) for here, k, size in zip(heres, steps, sizes)]
        block = blocks[tuple(slice(int(k), int(k) + 1) for k in steps)]
        out = lax.dynamic_update_slice(out, block, tuple(at) + (0,) * rest)
    return out


def scatter_sum(own, others, axis):
    count = lax.axis_size(axis)
    total = own.astype(jnp.float32)
    for step in range(1, count):
        got = lax.ppermute(
            others[step - 1].astype(jnp.bfloat16), axis, [(i, (i + step) % count) for i in range(count)]
        )
        total = total + got.astype(jnp.float32)
    return total


def by_distance(values, axis):
    count = lax.axis_size(axis)
    here = lax.axis_index(axis)
    return [
        lax.dynamic_index_in_dim(values, lax.rem(here + step, count), 0, keepdims=False)
        for step in range(count)
    ]


def exchange(values):
    return lax.all_to_all(values, CHIPS, split_axis=0, concat_axis=0, tiled=True)


def body(tokens, expert_ids, gate_code, grad_out, up_weight, down_weight, shared_up, shared_down):
    core = lax.axis_index("core")
    rows, width = tokens.shape
    chips = lax.axis_size("z") * lax.axis_size("ylo") * lax.axis_size("x") * lax.axis_size("yhi")
    cap = 4 * rows // (2 * chips)
    slots = chips * 2 * cap

    hidden_rows = shared_down.shape[0]
    groups = shared_up.shape[1] // (2 * hidden_rows)
    half = groups * hidden_rows
    unit = jnp.arange(2 * half, dtype=jnp.int32)
    inner = lax.rem(unit, half)
    side = jnp.where(unit < half, core, 1 - core)
    picked = (inner // hidden_rows * 2 + side) * hidden_rows + lax.rem(inner, hidden_rows)
    picking = (unit[:, None] == picked[None, :]).astype(jnp.bfloat16)
    by_core = dot(shared_up, picking).astype(jnp.bfloat16)
    up_keep, up_send = by_core[:, :half], by_core[:, half:]
    up_near = swap(up_send)
    up_far = lax.ppermute(up_keep, "yhi", [(0, 1), (1, 0)])
    up_cross = lax.ppermute(up_send, ("yhi", "core"), [(i, 3 - i) for i in range(4)])

    quarters, x_count, yhi_count = lax.axis_size("z"), lax.axis_size("x"), lax.axis_size("yhi")
    few = hidden_rows // quarters
    piece = lax.dynamic_slice_in_dim(shared_down, lax.axis_index("z") * few, few, 0)
    piece = collect(piece, "yhi")
    expert_ids, piece, tokens_other, up_near, up_far, up_cross, grad_out = together(
        expert_ids, piece, swap(tokens), up_near, up_far, up_cross, grad_out
    )
    grads_other = swap(grad_out)
    piece = collect(piece, "x")

    def by_rows(same, other):
        return jnp.where(
            core == 0,
            jnp.concatenate([same, other], axis=0),
            jnp.concatenate([other, same], axis=0),
        )

    up_pair = jnp.stack([by_rows(up_keep, up_near), by_rows(up_far, up_cross)])
    up_full = collect(up_pair, "x")

    chip_tokens = jnp.concatenate([tokens, tokens_other], axis=0)
    chip_grads = jnp.concatenate([grad_out, grads_other], axis=0)

    id_rows = expert_ids.T
    order = jnp.arange(rows, dtype=jnp.int32)
    earlier = order[:, None] < order[None, :]
    positions = []
    for column in range(2):
        same = (expert_ids[:, 0:1] == id_rows[column : column + 1]) | (
            expert_ids[:, 1:2] == id_rows[column : column + 1]
        )
        positions.append(jnp.sum((same & earlier).astype(jnp.int32), axis=0))
    routes = jnp.stack(
        [id_rows[0] * cap + positions[0], id_rows[1] * cap + positions[1], gate_code]
    )
    routes_other = swap(routes)

    def targets(packed, offset):
        expert = packed[:2] // cap
        position = packed[:2] - expert * cap
        slot = (expert // 2) * (2 * cap) + offset + position
        return jnp.where(expert - (expert // 2) * 2 == core, slot, -1)

    target = jnp.concatenate([targets(routes, 0), targets(routes_other, cap)], axis=1)
    first_gate = jnp.concatenate([routes[2], routes_other[2]]).astype(jnp.float32) / 8.0
    slot_grid = jnp.arange(slots, dtype=jnp.int32)[:, None]
    hit_first = slot_grid == target[0][None, :]
    hit_second = slot_grid == target[1][None, :]
    placing = (hit_first | hit_second).astype(jnp.bfloat16)
    weighing = (
        jnp.where(hit_first, first_gate[None, :], 0.0)
        + jnp.where(hit_second, 1.0 - first_gate[None, :], 0.0)
    ).astype(jnp.bfloat16)

    chip_tokens, chip_grads, piece = together(chip_tokens, chip_grads, piece)
    payload = dot(placing, chip_tokens).astype(jnp.bfloat16)
    arrived = exchange(payload)
    quarter, after, opposite, before = pieces(piece, "z")
    chip_grads, up_full, after, before = together(chip_grads, up_full, after, before)
    upstream = exchange(dot(weighing, chip_grads).astype(jnp.bfloat16))
    shared_in = in_order(up_full, ("x", "yhi")).reshape(width, half)
    shared_back_out = jnp.stack([quarter, after, opposite, before]).reshape(half, width)

    arrived, shared_in, shared_back_out = together(arrived, shared_in, shared_back_out)

    place = jnp.arange(half, dtype=jnp.int32)
    sizes = (quarters, x_count, yhi_count, few)
    steps = []
    for size in reversed(sizes):
        steps.append(lax.rem(place, size))
        place = place // size
    row, on_yhi, on_x, on_z = steps
    on_yhi = lax.rem(on_yhi + lax.axis_index("yhi"), yhi_count)
    on_x = lax.rem(on_x + lax.axis_index("x"), x_count)
    on_z = lax.rem(on_z + lax.axis_index("z"), quarters)
    natural = ((on_x * yhi_count + on_yhi) * quarters + on_z) * few + row
    turning = (jnp.arange(half, dtype=jnp.int32)[:, None] == natural[None, :]).astype(jnp.bfloat16)
    turned_in = dot(shared_in, turning).astype(jnp.bfloat16)

    shared_pre = dot(chip_tokens, turned_in)
    shared_hidden = gelu_value(shared_pre).astype(jnp.bfloat16)
    shared_back = contract_cols(chip_grads, shared_back_out)
    shared_slopes = (shared_back * gelu_slope(shared_pre)).astype(jnp.bfloat16)
    term_out = contract_rows(shared_hidden, chip_grads).astype(jnp.bfloat16)
    natural_slopes = contract_cols(shared_slopes, turning).astype(jnp.bfloat16)
    term_in = contract_rows(chip_tokens, natural_slopes).astype(jnp.bfloat16)

    near_in, *far_in = by_distance(term_in.reshape(x_count, -1, half), "x")
    part_in = scatter_sum(near_in, far_in, "x")
    term_out = term_out.reshape(quarters, -1, width)
    part_out = scatter_sum(term_out[0], term_out[1:], "z")

    upward = up_weight[0]
    downward = down_weight[0]
    preact = dot(arrived, upward)
    hidden = gelu_value(preact).astype(jnp.bfloat16)
    produced = dot(hidden, downward).astype(jnp.bfloat16)
    returned = exchange(produced)
    upstream, part_in, part_out = together(upstream, part_in, part_out)
    hidden_grad = contract_cols(upstream, downward)
    slopes = (hidden_grad * gelu_slope(preact)).astype(jnp.bfloat16)
    inward = contract_cols(slopes, upward).astype(jnp.bfloat16)

    part_in = part_in.reshape(yhi_count, 2, quarters, -1, half).transpose(2, 0, 1, 3, 4)
    near_in, *far_in = by_distance(part_in, "z")
    part_in = scatter_sum(near_in, far_in, "z").reshape(yhi_count, -1, half)
    part_out = part_out.reshape(x_count, yhi_count, -1, width)
    part_out = scatter_sum(part_out[0], part_out[1:], "x")
    part_in = jnp.stack(by_distance(part_in, "yhi"))
    part = jnp.stack([part_in, part_out.reshape(part_in.shape)], axis=1).astype(jnp.bfloat16)

    part, inward = together(part, inward)

    along_y = ("ylo", "yhi")
    ring = count_of(along_y)
    here = place_of(along_y)
    parts = jnp.zeros((ring,) + part.shape[1:], part.dtype)
    for step in range(ring):
        target = lax.rem(here + step, ring)
        got = lax.dynamic_index_in_dim(
            part, lax.rem(target + here, yhi_count), 0, keepdims=False
        )
        if step:
            got = lax.ppermute(got, along_y, [(i, (i + step) % ring) for i in range(ring)])
        origin = lax.rem(here + ring - step, ring)
        parts = lax.dynamic_update_slice(parts, got[None], (origin, 0, 0, 0))
    parts = parts.astype(jnp.float32).sum(axis=0).astype(jnp.bfloat16)
    inward, parts, returned = together(inward, parts, returned)
    landed = exchange(inward)

    parts = in_order(collect(parts, "z"), ("z",))
    parts, returned, upstream, shared_hidden, shared_slopes = together(
        parts, returned, upstream, shared_hidden, shared_slopes
    )
    sum_out = parts[:, 1].reshape(shared_down.shape).astype(jnp.float32)
    both = parts[:, 0].reshape(quarters, 2, -1, half).swapaxes(0, 1).reshape(2, -1, half)
    in_keep = lax.dynamic_index_in_dim(both, core, 0, keepdims=False)
    in_got = swap(lax.dynamic_index_in_dim(both, 1 - core, 0, keepdims=False))
    sum_in = contract_cols(jnp.concatenate([in_keep, in_got], axis=1), picking)

    def parts_of(routing, rows_back, shared_part):
        near = contract_rows(routing[:, :rows], rows_back) + shared_part[:rows]
        far = contract_rows(routing[:, rows:], rows_back) + shared_part[rows:]
        return near, far.astype(jnp.bfloat16)

    def whole(near, far):
        return (near + swap(far).astype(jnp.float32)).astype(jnp.bfloat16)

    out_near, out_far = parts_of(weighing, returned, dot(shared_hidden, shared_back_out))
    shared_grad = contract_cols(shared_slopes, turned_in)
    out_near, out_far, shared_grad, slopes = together(out_near, out_far, shared_grad, slopes)
    grad_upper = contract_rows(arrived, slopes).astype(jnp.bfloat16)
    grad_lower = contract_rows(hidden, upstream).astype(jnp.bfloat16)
    landed, grad_upper, grad_lower = together(landed, grad_upper, grad_lower)
    grad_near, grad_far = parts_of(placing, landed, shared_grad)
    layer_out = whole(out_near, out_far)
    grad_tokens = whole(grad_near, grad_far)
    return (layer_out, grad_tokens, grad_upper[None], grad_lower[None], sum_in, sum_out)


def solution(mesh):
    node, local = mesh.shape["node"], mesh.shape["local"]
    fine = Mesh(mesh.devices.reshape(node // 2, 2, local // 4, 2, 2), AXES)
    every = AXES
    shared = ("x", "yhi", "core")
    return jax.shard_map(
        body,
        mesh=fine,
        in_specs=(
            P(every, None),
            P(every, None),
            P(every),
            P(every, None),
            P(every, None, None),
            P(every, None, None),
            P(shared, None),
            P(shared, None),
        ),
        out_specs=(
            P(every, None),
            P(every, None),
            P(every, None, None),
            P(every, None, None),
            P(shared, None),
            P(shared, None),
        ),
        check_vma=False,
    )
```

```python
import math

import numpy as np
import jax
import jax.numpy as jnp
from jax import lax
from jax.sharding import Mesh, PartitionSpec as P

half_root = 0.7071067811865476
inv_root_tau = 0.3989422804014327

AXES = ("z", "ylo", "x", "yhi", "core")
CHIPS = ("z", "ylo", "x", "yhi")


def gelu_value(values):
    return 0.5 * values * (1.0 + lax.erf(values * half_root))


def gelu_slope(values):
    return 0.5 * (1.0 + lax.erf(values * half_root)) + values * inv_root_tau * jnp.exp(
        -0.5 * values * values
    )


def dot(left, right):
    return jnp.dot(left, right, preferred_element_type=jnp.float32)


def contract_rows(left, right):
    return lax.dot_general(
        left, right, (((0,), (0,)), ((), ())), preferred_element_type=jnp.float32
    )


def contract_cols(left, right):
    return lax.dot_general(
        left, right, (((1,), (1,)), ((), ())), preferred_element_type=jnp.float32
    )


def together(*arrays):
    return lax.optimization_barrier(arrays)


def swap(values):
    return lax.ppermute(values, "core", [(0, 1), (1, 0)])


def place_of(axes):
    place = 0
    for axis in axes:
        place = place * lax.axis_size(axis) + lax.axis_index(axis)
    return place


def count_of(axes):
    count = 1
    for axis in axes:
        count *= lax.axis_size(axis)
    return count


def pieces(values, axis):
    count = lax.axis_size(axis)
    return [values] + [
        lax.ppermute(values, axis, [((i + step) % count, i) for i in range(count)])
        for step in range(1, count)
    ]


def collect(values, axis):
    return jnp.stack(pieces(values, axis))


def in_order(blocks, axes):
    sizes = [lax.axis_size(axis) for axis in axes]
    heres = [lax.axis_index(axis) for axis in axes]
    out = jnp.zeros_like(blocks)
    rest = blocks.ndim - len(axes)
    for index in range(math.prod(sizes)):
        steps = np.unravel_index(index, sizes)
        at = [lax.rem(here + int(k), size) for here, k, size in zip(heres, steps, sizes)]
        block = blocks[tuple(slice(int(k), int(k) + 1) for k in steps)]
        out = lax.dynamic_update_slice(out, block, tuple(at) + (0,) * rest)
    return out


def scatter_sum(own, others, axis):
    count = lax.axis_size(axis)
    total = own.astype(jnp.float32)
    for step in range(1, count):
        got = lax.ppermute(
            others[step - 1].astype(jnp.bfloat16), axis, [(i, (i + step) % count) for i in range(count)]
        )
        total = total + got.astype(jnp.float32)
    return total


def by_distance(values, axis):
    count = lax.axis_size(axis)
    here = lax.axis_index(axis)
    return [
        lax.dynamic_index_in_dim(values, lax.rem(here + step, count), 0, keepdims=False)
        for step in range(count)
    ]


def exchange(values):
    return lax.all_to_all(values, CHIPS, split_axis=0, concat_axis=0, tiled=True)


def body(tokens, expert_ids, gate_code, grad_out, up_weight, down_weight, shared_up, shared_down):
    core = lax.axis_index("core")
    rows, width = tokens.shape
    chips = lax.axis_size("z") * lax.axis_size("ylo") * lax.axis_size("x") * lax.axis_size("yhi")
    cap = 4 * rows // (2 * chips)
    slots = chips * 2 * cap

    hidden_rows = shared_down.shape[0]
    groups = shared_up.shape[1] // (2 * hidden_rows)
    half = groups * hidden_rows
    unit = jnp.arange(2 * half, dtype=jnp.int32)
    inner = lax.rem(unit, half)
    side = jnp.where(unit < half, core, 1 - core)
    picked = (inner // hidden_rows * 2 + side) * hidden_rows + lax.rem(inner, hidden_rows)
    picking = (unit[:, None] == picked[None, :]).astype(jnp.bfloat16)
    by_core = dot(shared_up, picking).astype(jnp.bfloat16)
    up_keep, up_send = by_core[:, :half], by_core[:, half:]
    up_near = swap(up_send)
    up_far = lax.ppermute(up_keep, "yhi", [(0, 1), (1, 0)])
    up_cross = lax.ppermute(up_send, ("yhi", "core"), [(i, 3 - i) for i in range(4)])

    quarters, x_count, yhi_count = lax.axis_size("z"), lax.axis_size("x"), lax.axis_size("yhi")
    few = hidden_rows // quarters
    piece = lax.dynamic_slice_in_dim(shared_down, lax.axis_index("z") * few, few, 0)
    piece = collect(piece, "yhi")
    expert_ids, piece, tokens_other, up_near, up_far, up_cross, grad_out = together(
        expert_ids, piece, swap(tokens), up_near, up_far, up_cross, grad_out
    )
    grads_other = swap(grad_out)
    piece = collect(piece, "x")

    def by_rows(same, other):
        return jnp.where(
            core == 0,
            jnp.concatenate([same, other], axis=0),
            jnp.concatenate([other, same], axis=0),
        )

    up_pair = jnp.stack([by_rows(up_keep, up_near), by_rows(up_far, up_cross)])
    up_full = collect(up_pair, "x")

    chip_tokens = jnp.concatenate([tokens, tokens_other], axis=0)
    chip_grads = jnp.concatenate([grad_out, grads_other], axis=0)

    id_rows = expert_ids.T
    order = jnp.arange(rows, dtype=jnp.int32)
    earlier = order[:, None] < order[None, :]
    positions = []
    for column in range(2):
        same = (expert_ids[:, 0:1] == id_rows[column : column + 1]) | (
            expert_ids[:, 1:2] == id_rows[column : column + 1]
        )
        positions.append(jnp.sum((same & earlier).astype(jnp.int32), axis=0))
    routes = jnp.stack(
        [id_rows[0] * cap + positions[0], id_rows[1] * cap + positions[1], gate_code]
    )
    routes_other = swap(routes)

    def targets(packed, offset):
        expert = packed[:2] // cap
        position = packed[:2] - expert * cap
        slot = (expert // 2) * (2 * cap) + offset + position
        return jnp.where(expert - (expert // 2) * 2 == core, slot, -1)

    target = jnp.concatenate([targets(routes, 0), targets(routes_other, cap)], axis=1)
    first_gate = jnp.concatenate([routes[2], routes_other[2]]).astype(jnp.float32) / 8.0
    slot_grid = jnp.arange(slots, dtype=jnp.int32)[:, None]
    hit_first = slot_grid == target[0][None, :]
    hit_second = slot_grid == target[1][None, :]
    placing = (hit_first | hit_second).astype(jnp.bfloat16)
    weighing = (
        jnp.where(hit_first, first_gate[None, :], 0.0)
        + jnp.where(hit_second, 1.0 - first_gate[None, :], 0.0)
    ).astype(jnp.bfloat16)

    chip_tokens, chip_grads, piece = together(chip_tokens, chip_grads, piece)
    payload = dot(placing, chip_tokens).astype(jnp.bfloat16)
    arrived = exchange(payload)
    quarter, after, opposite, before = pieces(piece, "z")
    chip_grads, up_full, after, before = together(chip_grads, up_full, after, before)
    weighed = dot(weighing, chip_grads).astype(jnp.bfloat16)
    shared_in = in_order(up_full, ("x", "yhi")).reshape(width, half)

    place = jnp.arange(half, dtype=jnp.int32)
    sizes = (quarters, x_count, yhi_count, few)
    steps = []
    for size in reversed(sizes):
        steps.append(lax.rem(place, size))
        place = place // size
    row, on_yhi, on_x, on_z = steps
    on_yhi = lax.rem(on_yhi + lax.axis_index("yhi"), yhi_count)
    on_x = lax.rem(on_x + lax.axis_index("x"), x_count)
    on_z = lax.rem(on_z + lax.axis_index("z"), quarters)
    natural = ((on_x * yhi_count + on_yhi) * quarters + on_z) * few + row
    turning = (jnp.arange(half, dtype=jnp.int32)[:, None] == natural[None, :]).astype(jnp.bfloat16)
    turned_in = dot(shared_in, turning).astype(jnp.bfloat16)

    shared_pre = dot(chip_tokens, turned_in)
    shared_hidden = gelu_value(shared_pre).astype(jnp.bfloat16)
    term_out = contract_rows(shared_hidden, chip_grads).astype(jnp.bfloat16)
    opposite, shared_pre, shared_hidden, term_out, weighed = together(
        opposite, shared_pre, shared_hidden, term_out, weighed
    )
    upstream = exchange(weighed)
    shared_back_out = jnp.stack([quarter, after, opposite, before]).reshape(half, width)
    arrived, shared_back_out, term_out = together(arrived, shared_back_out, term_out)
    shared_back = contract_cols(chip_grads, shared_back_out)
    shared_slopes = (shared_back * gelu_slope(shared_pre)).astype(jnp.bfloat16)
    natural_slopes = contract_cols(shared_slopes, turning).astype(jnp.bfloat16)
    term_in = contract_rows(chip_tokens, natural_slopes).astype(jnp.bfloat16)

    near_in, *far_in = by_distance(term_in.reshape(x_count, -1, half), "x")
    part_in = scatter_sum(near_in, far_in, "x")
    term_out = term_out.reshape(quarters, -1, width)
    part_out = scatter_sum(term_out[0], term_out[1:], "z")

    upward = up_weight[0]
    downward = down_weight[0]
    preact = dot(arrived, upward)
    hidden = gelu_value(preact).astype(jnp.bfloat16)
    produced = dot(hidden, downward).astype(jnp.bfloat16)
    returned = exchange(produced)
    upstream, part_in, part_out = together(upstream, part_in, part_out)
    hidden_grad = contract_cols(upstream, downward)
    slopes = (hidden_grad * gelu_slope(preact)).astype(jnp.bfloat16)
    inward = contract_cols(slopes, upward).astype(jnp.bfloat16)

    part_in = part_in.reshape(yhi_count, 2, quarters, -1, half).transpose(2, 0, 1, 3, 4)
    near_in, *far_in = by_distance(part_in, "z")
    part_in = scatter_sum(near_in, far_in, "z").reshape(yhi_count, -1, half)
    part_out = part_out.reshape(x_count, yhi_count, -1, width)
    part_out = scatter_sum(part_out[0], part_out[1:], "x")
    part_in = jnp.stack(by_distance(part_in, "yhi"))
    part = jnp.stack([part_in, part_out.reshape(part_in.shape)], axis=1).astype(jnp.bfloat16)

    shared_result = dot(shared_hidden, shared_back_out)
    shared_grad = contract_cols(shared_slopes, turned_in)
    part, inward, shared_result, shared_grad = together(part, inward, shared_result, shared_grad)

    along_y = ("ylo", "yhi")
    ring = count_of(along_y)
    here = place_of(along_y)
    parts = jnp.zeros((ring,) + part.shape[1:], part.dtype)
    for step in range(ring):
        target = lax.rem(here + step, ring)
        got = lax.dynamic_index_in_dim(
            part, lax.rem(target + here, yhi_count), 0, keepdims=False
        )
        if step:
            got = lax.ppermute(got, along_y, [(i, (i + step) % ring) for i in range(ring)])
        origin = lax.rem(here + ring - step, ring)
        parts = lax.dynamic_update_slice(parts, got[None], (origin, 0, 0, 0))
    parts = parts.astype(jnp.float32).sum(axis=0).astype(jnp.bfloat16)
    inward, parts, returned = together(inward, parts, returned)
    landed = exchange(inward)

    parts = in_order(collect(parts, "z"), ("z",))
    parts, returned, upstream, slopes = together(parts, returned, upstream, slopes)
    sum_out = parts[:, 1].reshape(shared_down.shape).astype(jnp.float32)
    both = parts[:, 0].reshape(quarters, 2, -1, half).swapaxes(0, 1).reshape(2, -1, half)
    in_keep = lax.dynamic_index_in_dim(both, core, 0, keepdims=False)
    in_got = swap(lax.dynamic_index_in_dim(both, 1 - core, 0, keepdims=False))
    sum_in = contract_cols(jnp.concatenate([in_keep, in_got], axis=1), picking)

    def parts_of(routing, rows_back, shared_part):
        near = contract_rows(routing[:, :rows], rows_back) + shared_part[:rows]
        far = contract_rows(routing[:, rows:], rows_back) + shared_part[rows:]
        return near, far.astype(jnp.bfloat16)

    def whole(near, far):
        return (near + swap(far).astype(jnp.float32)).astype(jnp.bfloat16)

    layer_out = whole(*parts_of(weighing, returned, shared_result))
    grad_upper = contract_rows(arrived, slopes).astype(jnp.bfloat16)
    grad_lower = contract_rows(hidden, upstream).astype(jnp.bfloat16)
    landed, grad_upper, grad_lower, layer_out, sum_in, sum_out = together(
        landed, grad_upper, grad_lower, layer_out, sum_in, sum_out
    )
    grad_tokens = whole(*parts_of(placing, landed, shared_grad))
    return (layer_out, grad_tokens, grad_upper[None], grad_lower[None], sum_in, sum_out)


def solution(mesh):
    node, local = mesh.shape["node"], mesh.shape["local"]
    fine = Mesh(mesh.devices.reshape(node // 2, 2, local // 4, 2, 2), AXES)
    every = AXES
    shared = ("x", "yhi", "core")
    return jax.shard_map(
        body,
        mesh=fine,
        in_specs=(
            P(every, None),
            P(every, None),
            P(every),
            P(every, None),
            P(every, None, None),
            P(every, None, None),
            P(shared, None),
            P(shared, None),
        ),
        out_specs=(
            P(every, None),
            P(every, None),
            P(every, None, None),
            P(every, None, None),
            P(shared, None),
            P(shared, None),
        ),
        check_vma=False,
    )
```

```python
import math

import numpy as np
import jax
import jax.numpy as jnp
from jax import lax
from jax.sharding import Mesh, PartitionSpec as P

half_root = 0.7071067811865476
inv_root_tau = 0.3989422804014327

AXES = ("z", "ylo", "x", "yhi", "core")
CHIPS = ("z", "ylo", "x", "yhi")


def gelu_value(values):
    return 0.5 * values * (1.0 + lax.erf(values * half_root))


def gelu_slope(values):
    return 0.5 * (1.0 + lax.erf(values * half_root)) + values * inv_root_tau * jnp.exp(
        -0.5 * values * values
    )


def dot(left, right):
    return jnp.dot(left, right, preferred_element_type=jnp.float32)


def contract_rows(left, right):
    return lax.dot_general(
        left, right, (((0,), (0,)), ((), ())), preferred_element_type=jnp.float32
    )


def contract_cols(left, right):
    return lax.dot_general(
        left, right, (((1,), (1,)), ((), ())), preferred_element_type=jnp.float32
    )


def together(*arrays):
    return lax.optimization_barrier(arrays)


def swap(values):
    return lax.ppermute(values, "core", [(0, 1), (1, 0)])


def place_of(axes):
    place = 0
    for axis in axes:
        place = place * lax.axis_size(axis) + lax.axis_index(axis)
    return place


def count_of(axes):
    count = 1
    for axis in axes:
        count *= lax.axis_size(axis)
    return count


def pieces(values, axis):
    count = lax.axis_size(axis)
    return [values] + [
        lax.ppermute(values, axis, [((i + step) % count, i) for i in range(count)])
        for step in range(1, count)
    ]


def collect(values, axis):
    return jnp.stack(pieces(values, axis))


def in_order(blocks, axes):
    sizes = [lax.axis_size(axis) for axis in axes]
    heres = [lax.axis_index(axis) for axis in axes]
    out = jnp.zeros_like(blocks)
    rest = blocks.ndim - len(axes)
    for index in range(math.prod(sizes)):
        steps = np.unravel_index(index, sizes)
        at = [lax.rem(here + int(k), size) for here, k, size in zip(heres, steps, sizes)]
        block = blocks[tuple(slice(int(k), int(k) + 1) for k in steps)]
        out = lax.dynamic_update_slice(out, block, tuple(at) + (0,) * rest)
    return out


def scatter_sum(own, others, axis):
    count = lax.axis_size(axis)
    total = own.astype(jnp.float32)
    for step in range(1, count):
        got = lax.ppermute(
            others[step - 1].astype(jnp.bfloat16), axis, [(i, (i + step) % count) for i in range(count)]
        )
        total = total + got.astype(jnp.float32)
    return total


def by_distance(values, axis):
    count = lax.axis_size(axis)
    here = lax.axis_index(axis)
    return [
        lax.dynamic_index_in_dim(values, lax.rem(here + step, count), 0, keepdims=False)
        for step in range(count)
    ]


def exchange(values):
    return lax.all_to_all(values, CHIPS, split_axis=0, concat_axis=0, tiled=True)


def body(tokens, expert_ids, gate_code, grad_out, up_weight, down_weight, shared_up, shared_down):
    core = lax.axis_index("core")
    rows, width = tokens.shape
    chips = lax.axis_size("z") * lax.axis_size("ylo") * lax.axis_size("x") * lax.axis_size("yhi")
    cap = 4 * rows // (2 * chips)
    slots = chips * 2 * cap

    hidden_rows = shared_down.shape[0]
    groups = shared_up.shape[1] // (2 * hidden_rows)
    half = groups * hidden_rows
    unit = jnp.arange(2 * half, dtype=jnp.int32)
    inner = lax.rem(unit, half)
    side = jnp.where(unit < half, core, 1 - core)
    picked = (inner // hidden_rows * 2 + side) * hidden_rows + lax.rem(inner, hidden_rows)
    picking = (unit[:, None] == picked[None, :]).astype(jnp.bfloat16)
    by_core = dot(shared_up, picking).astype(jnp.bfloat16)
    up_keep, up_send = by_core[:, :half], by_core[:, half:]
    up_near = swap(up_send)
    up_far = lax.ppermute(up_keep, "yhi", [(0, 1), (1, 0)])
    up_cross = lax.ppermute(up_send, ("yhi", "core"), [(i, 3 - i) for i in range(4)])

    quarters, x_count, yhi_count = lax.axis_size("z"), lax.axis_size("x"), lax.axis_size("yhi")
    few = hidden_rows // quarters
    piece = lax.dynamic_slice_in_dim(shared_down, lax.axis_index("z") * few, few, 0)
    piece = collect(piece, "yhi")
    expert_ids, piece, tokens_other, up_near, up_far, up_cross, grad_out = together(
        expert_ids, piece, swap(tokens), up_near, up_far, up_cross, grad_out
    )
    grads_other = swap(grad_out)
    piece = collect(piece, "x")

    def by_rows(same, other):
        return jnp.where(
            core == 0,
            jnp.concatenate([same, other], axis=0),
            jnp.concatenate([other, same], axis=0),
        )

    up_pair = jnp.stack([by_rows(up_keep, up_near), by_rows(up_far, up_cross)])
    up_full = collect(up_pair, "x")

    chip_tokens = jnp.concatenate([tokens, tokens_other], axis=0)
    chip_grads = jnp.concatenate([grad_out, grads_other], axis=0)

    id_rows = expert_ids.T
    order = jnp.arange(rows, dtype=jnp.int32)
    earlier = order[:, None] < order[None, :]
    positions = []
    for column in range(2):
        same = (expert_ids[:, 0:1] == id_rows[column : column + 1]) | (
            expert_ids[:, 1:2] == id_rows[column : column + 1]
        )
        positions.append(jnp.sum((same & earlier).astype(jnp.int32), axis=0))
    routes = jnp.stack(
        [id_rows[0] * cap + positions[0], id_rows[1] * cap + positions[1], gate_code]
    )
    routes_other = swap(routes)

    def targets(packed, offset):
        expert = packed[:2] // cap
        position = packed[:2] - expert * cap
        slot = (expert // 2) * (2 * cap) + offset + position
        return jnp.where(expert - (expert // 2) * 2 == core, slot, -1)

    target = jnp.concatenate([targets(routes, 0), targets(routes_other, cap)], axis=1)
    first_gate = jnp.concatenate([routes[2], routes_other[2]]).astype(jnp.float32) / 8.0
    slot_grid = jnp.arange(slots, dtype=jnp.int32)[:, None]
    hit_first = slot_grid == target[0][None, :]
    hit_second = slot_grid == target[1][None, :]
    placing = (hit_first | hit_second).astype(jnp.bfloat16)
    weighing = (
        jnp.where(hit_first, first_gate[None, :], 0.0)
        + jnp.where(hit_second, 1.0 - first_gate[None, :], 0.0)
    ).astype(jnp.bfloat16)

    chip_tokens, chip_grads, piece = together(chip_tokens, chip_grads, piece)
    payload = dot(placing, chip_tokens).astype(jnp.bfloat16)
    arrived = exchange(payload)
    quarter, after, opposite, before = pieces(piece, "z")
    chip_grads, up_full, after, before = together(chip_grads, up_full, after, before)
    upstream = exchange(dot(weighing, chip_grads).astype(jnp.bfloat16))
    shared_in = in_order(up_full, ("x", "yhi")).reshape(width, half)
    shared_back_out = jnp.stack([quarter, after, opposite, before]).reshape(half, width)

    arrived, shared_in, shared_back_out = together(arrived, shared_in, shared_back_out)

    place = jnp.arange(half, dtype=jnp.int32)
    sizes = (quarters, x_count, yhi_count, few)
    steps = []
    for size in reversed(sizes):
        steps.append(lax.rem(place, size))
        place = place // size
    row, on_yhi, on_x, on_z = steps
    on_yhi = lax.rem(on_yhi + lax.axis_index("yhi"), yhi_count)
    on_x = lax.rem(on_x + lax.axis_index("x"), x_count)
    on_z = lax.rem(on_z + lax.axis_index("z"), quarters)
    natural = ((on_x * yhi_count + on_yhi) * quarters + on_z) * few + row
    turning = (jnp.arange(half, dtype=jnp.int32)[:, None] == natural[None, :]).astype(jnp.bfloat16)
    turned_in = dot(shared_in, turning).astype(jnp.bfloat16)

    shared_pre = dot(chip_tokens, turned_in)
    shared_hidden = gelu_value(shared_pre).astype(jnp.bfloat16)
    shared_back = contract_cols(chip_grads, shared_back_out)
    shared_slopes = (shared_back * gelu_slope(shared_pre)).astype(jnp.bfloat16)
    term_out = contract_rows(shared_hidden, chip_grads).astype(jnp.bfloat16)
    natural_slopes = contract_cols(shared_slopes, turning).astype(jnp.bfloat16)
    term_in = contract_rows(chip_tokens, natural_slopes).astype(jnp.bfloat16)

    near_in, *far_in = by_distance(term_in.reshape(x_count, -1, half), "x")
    part_in = scatter_sum(near_in, far_in, "x")
    term_out = term_out.reshape(quarters, -1, width)
    part_out = scatter_sum(term_out[0], term_out[1:], "z")

    upward = up_weight[0]
    downward = down_weight[0]
    preact = dot(arrived, upward)
    hidden = gelu_value(preact).astype(jnp.bfloat16)
    produced = dot(hidden, downward).astype(jnp.bfloat16)
    returned = exchange(produced)
    upstream, part_in, part_out = together(upstream, part_in, part_out)
    hidden_grad = contract_cols(upstream, downward)
    slopes = (hidden_grad * gelu_slope(preact)).astype(jnp.bfloat16)
    inward = contract_cols(slopes, upward).astype(jnp.bfloat16)

    part_in = part_in.reshape(yhi_count, 2, quarters, -1, half).transpose(2, 0, 1, 3, 4)
    near_in, *far_in = by_distance(part_in, "z")
    part_in = scatter_sum(near_in, far_in, "z").reshape(yhi_count, -1, half)
    part_out = part_out.reshape(x_count, yhi_count, -1, width)
    part_out = scatter_sum(part_out[0], part_out[1:], "x")
    part_in = jnp.stack(by_distance(part_in, "yhi"))
    part = jnp.stack([part_in, part_out.reshape(part_in.shape)], axis=1).astype(jnp.bfloat16)

    part, inward = together(part, inward)

    along_y = ("ylo", "yhi")
    ring = count_of(along_y)
    here = place_of(along_y)
    parts = jnp.zeros((ring,) + part.shape[1:], part.dtype)
    for step in range(ring):
        target = lax.rem(here + step, ring)
        got = lax.dynamic_index_in_dim(
            part, lax.rem(target + here, yhi_count), 0, keepdims=False
        )
        if step:
            got = lax.ppermute(got, along_y, [(i, (i + step) % ring) for i in range(ring)])
        origin = lax.rem(here + ring - step, ring)
        parts = lax.dynamic_update_slice(parts, got[None], (origin, 0, 0, 0))
    parts = parts.astype(jnp.float32).sum(axis=0).astype(jnp.bfloat16)
    inward, parts, returned = together(inward, parts, returned)
    landed = exchange(inward)

    parts = in_order(collect(parts, "z"), ("z",))
    parts, returned, upstream, shared_hidden, shared_slopes = together(
        parts, returned, upstream, shared_hidden, shared_slopes
    )
    sum_out = parts[:, 1].reshape(shared_down.shape).astype(jnp.float32)
    both = parts[:, 0].reshape(quarters, 2, -1, half).swapaxes(0, 1).reshape(2, -1, half)
    in_keep = lax.dynamic_index_in_dim(both, core, 0, keepdims=False)
    in_got = swap(lax.dynamic_index_in_dim(both, 1 - core, 0, keepdims=False))

    def parts_of(routing, rows_back, shared_part):
        near = contract_rows(routing[:, :rows], rows_back) + shared_part[:rows]
        far = contract_rows(routing[:, rows:], rows_back) + shared_part[rows:]
        return near, far.astype(jnp.bfloat16)

    def whole(near, far):
        return (near + swap(far).astype(jnp.float32)).astype(jnp.bfloat16)

    out_near, out_far = parts_of(weighing, returned, dot(shared_hidden, shared_back_out))
    shared_grad = contract_cols(shared_slopes, turned_in)
    out_near, out_far, shared_grad, slopes = together(out_near, out_far, shared_grad, slopes)
    grad_upper = contract_rows(arrived, slopes).astype(jnp.bfloat16)
    grad_lower = contract_rows(hidden, upstream).astype(jnp.bfloat16)
    layer_out = whole(out_near, out_far)
    landed, grad_upper, grad_lower, layer_out, sum_out, in_keep, in_got = together(
        landed, grad_upper, grad_lower, layer_out, sum_out, in_keep, in_got
    )
    sum_in = contract_cols(jnp.concatenate([in_keep, in_got], axis=1), picking)
    grad_near, grad_far = parts_of(placing, landed, shared_grad)
    grad_tokens = whole(grad_near, grad_far)
    return (layer_out, grad_tokens, grad_upper[None], grad_lower[None], sum_in, sum_out)


def solution(mesh):
    node, local = mesh.shape["node"], mesh.shape["local"]
    fine = Mesh(mesh.devices.reshape(node // 2, 2, local // 4, 2, 2), AXES)
    every = AXES
    shared = ("x", "yhi", "core")
    return jax.shard_map(
        body,
        mesh=fine,
        in_specs=(
            P(every, None),
            P(every, None),
            P(every),
            P(every, None),
            P(every, None, None),
            P(every, None, None),
            P(shared, None),
            P(shared, None),
        ),
        out_specs=(
            P(every, None),
            P(every, None),
            P(every, None, None),
            P(every, None, None),
            P(shared, None),
            P(shared, None),
        ),
        check_vma=False,
    )
```
